512 devices in a mesh: band: 64 (over z_hi, y, core), dx: 4 (over x), dy: 2 (over z_lo).
Axes of the slice: x: 4, y: 8, z: 8 (z_hi: 4, z_lo: 2; z = z_hi * 2 + z_lo), core: 2. Of those that a mesh axis runs over, the one named last changes fastest.
Arguments:
- orbitals: bfloat16 [384, 64, 16, 128], P('band', 'dx', 'dy'), may hold values from -20 to 20
- potential: float32 [64, 16, 128], P('dx', 'dy'), may hold values from -6 to 6
Outputs:
- new_orbitals: bfloat16 [384, 64, 16, 128], P('band', 'dx', 'dy')
- subspace: float32 [384, 384], P(None, 'band')
The draws below stay inside these ranges and needn't reach their ends.
All inputs are finite; a program needn't handle non-finite values.
Results may differ from the reference program's by a relative error of at most 0.0068.
Values may be sent and summed in bfloat16 or wider, within the bound.
No kernel may reach another device: no remote copies, remote signals or barrier semaphores. Data moves between devices by JAX's collectives and lax.ppermute only.
A program may use at most 64 MiB of HBM per device.

```python
import math
import jax
import jax.numpy as jnp
from jax import lax

BANDS_DEV = 6
STEPS = 2
BANDS = 384
NX = 64
NY = 16
NZ = 128


def draw_orbitals(key, part):
    first, second, third = jax.random.split(key, 3)
    full_shape = (BANDS, NX, NY, NZ)
    noise = jnp.clip(jax.random.normal(first, full_shape, jnp.float32), -5.0, 5.0)
    envelope = jnp.exp(jax.random.uniform(second, (NX, NY, NZ), jnp.float32, math.log(0.3), math.log(3.0))) / 1.39
    gains = 1.0 + 0.1 * jax.random.uniform(third, (BANDS, 1, 1, 1), jnp.float32, -1.0, 1.0)
    mixed = noise + 0.25 * (jnp.roll(noise, -1, 0) + jnp.roll(noise, -37, 0) + jnp.roll(noise, -191, 0))
    return (mixed * envelope[None] * gains / 1.0897).astype(jnp.bfloat16)


def block_scale(key, extent, cuts, smallest, largest):
    def one(position, parts):
        draws = jax.random.uniform(jax.random.fold_in(jax.random.fold_in(key, 6), position), (parts,), jnp.float32, smallest / len(cuts), largest / len(cuts))
        return jnp.repeat(jnp.exp(draws), extent[position] // parts).reshape((-1,) + (1,) * (len(extent) - position - 1))

    gain = one(*cuts[0])
    for cut in cuts[1:]:
        gain = gain * one(*cut)
    return gain


def gaussian(rng, extent, width, limit, pieces=(), held_as=jnp.bfloat16):
    result = jax.random.normal(rng, extent, jnp.float32) * width
    if len(pieces) > 0:
        result = block_scale(rng, extent, pieces, -0.22, 0.18) * result
    return jnp.clip(result, min=-limit, max=limit).astype(held_as)


def setup_inputs(seed: int = 0) -> dict:
    splits = jax.random.split(jax.random.key(seed), 3)
    orbitals = draw_orbitals(jax.random.fold_in(splits[2], 71), 0)
    potential = gaussian(splits[1], (NX, NY, NZ), 1.0, 6.0, ((0, 4), (1, 2)), jnp.float32)
    return dict(orbitals=orbitals, potential=potential)


COEFFS = (-5369.0 / 1800.0, 12.0 / 7.0, -15.0 / 56.0, 10.0 / 189.0, -1.0 / 112.0, 2.0 / 1925.0, -1.0 / 16632.0)
TAU_STEP = 0.1


def laplacian(field):
    total = 3.0 * COEFFS[0] * field
    for offset in range(1, 7):
        total = total + COEFFS[offset] * (jnp.roll(field, offset, 1) + jnp.roll(field, -offset, 1) + jnp.roll(field, offset, 2) + jnp.roll(field, -offset, 2) + jnp.roll(field, offset, 3) + jnp.roll(field, -offset, 3))
    return total


def reference(orbitals, potential):
    volume = 1.0 / (NX * NY * NZ)
    groups = BANDS // BANDS_DEV
    psi = orbitals
    eye = jnp.eye(BANDS, dtype=jnp.float32)
    hsub = jnp.zeros((BANDS, BANDS), jnp.float32)

    def apply_hamiltonian(block):
        field = block.astype(jnp.float32)
        return (-0.5 * laplacian(field) + potential[None] * field).astype(jnp.bfloat16)

    for sweep in range(STEPS):
        image = lax.map(apply_hamiltonian, psi.reshape(groups, BANDS_DEV, NX, NY, NZ)).reshape(BANDS, NX * NY * NZ)
        flat = psi.reshape(BANDS, NX * NY * NZ)
        hsub = volume * lax.dot_general(flat, image, (((1,), (1,)), ((), ())), preferred_element_type=jnp.float32)
        h_rounded = hsub.astype(jnp.bfloat16)
        rotated = lax.dot_general(h_rounded, flat, (((0,), (0,)), ((), ())), preferred_element_type=jnp.float32)
        updated = flat.astype(jnp.float32) - TAU_STEP * image.astype(jnp.float32) + TAU_STEP * rotated
        correlation = volume * lax.dot_general(updated, updated, (((1,), (1,)), ((), ())), precision=lax.Precision.HIGHEST, preferred_element_type=jnp.float32)
        correction = 1.5 * eye - 0.5 * correlation
        fixed = lax.dot_general(correction, updated, (((0,), (0,)), ((), ())), precision=lax.Precision.HIGHEST, preferred_element_type=jnp.float32)
        psi = fixed.astype(jnp.bfloat16).reshape(BANDS, NX, NY, NZ)
    return psi, hsub
```

```python
import jax
import jax.numpy as jnp
from jax import lax
from jax.sharding import Mesh, PartitionSpec as P

COEFFS = (
    -5369.0 / 1800.0,
    12.0 / 7.0,
    -15.0 / 56.0,
    10.0 / 189.0,
    -1.0 / 112.0,
    2.0 / 1925.0,
    -1.0 / 16632.0,
)
TAU = 0.1
BF = jnp.bfloat16
F32 = jnp.float32
BAND = ("zhi", "y", "core")
CHIPS = ("zhi", "y")
DOMAINS = ("dx", "dy")
BLK = 128
NGRAM = 5


def halo(block):
    count = lax.axis_size("dx")
    up = [(i, (i + 1) % count) for i in range(count)]
    down = [(b, a) for a, b in up]
    other = lax.ppermute(block, "dy", [(0, 1), (1, 0)])
    low = lax.ppermute(block[:, block.shape[1] - 6 :], "dx", up)
    high = lax.ppermute(block[:, :6], "dx", down)
    return other, low, high


def hamiltonian(block, potential):
    other, low, high = halo(block)
    wx, wy = block.shape[1], block.shape[2]
    f = block.astype(F32)
    px = jnp.concatenate([low, block, high], axis=1).astype(F32)
    o = other.astype(F32)
    py = jnp.concatenate([o[:, :, wy - 6 :], f, o[:, :, :6]], axis=2)
    total = 3.0 * COEFFS[0] * f
    for k in range(1, 7):
        along_x = px[:, 6 + k : 6 + k + wx] + px[:, 6 - k : 6 - k + wx]
        along_y = py[:, :, 6 + k : 6 + k + wy] + py[:, :, 6 - k : 6 - k + wy]
        along_z = jnp.roll(f, k, 3) + jnp.roll(f, -k, 3)
        total = total + COEFFS[k] * (along_x + along_y + along_z)
    return (-0.5 * total + potential[None] * f).astype(BF)


def swap(x, axes):
    return lax.all_to_all(x, axes, split_axis=0, concat_axis=0, tiled=True)


def spread(x, axes, size):
    return swap(jnp.broadcast_to(x[None], (size,) + x.shape), axes)


def gram(a, b):
    return lax.dot_general(a, b, (((1,), (1,)), ((), ())), preferred_element_type=F32)


def pairs(nblk):
    return [(r, c) for r in range(nblk) for c in range(r, nblk)]


def pack(g):
    nblk = g.shape[0] // BLK
    return [g[r * BLK : (r + 1) * BLK, c * BLK : (c + 1) * BLK] for r, c in pairs(nblk)]


def unpack(blocks, nblk):
    at = dict(zip(pairs(nblk), blocks))
    rows = [
        jnp.concatenate([at[r, c] if r <= c else at[c, r].T for c in range(nblk)], axis=1)
        for r in range(nblk)
    ]
    return jnp.concatenate(rows, axis=0)


def mm(a, b):
    return lax.dot_general(
        a, b, (((1,), (0,)), ((), ())), precision=lax.Precision.HIGH, preferred_element_type=F32
    )


def reduced(rows):
    n_core, n_dom, n_chip = (
        lax.axis_size("core"),
        lax.axis_size("dx") * lax.axis_size("dy"),
        lax.axis_size("zhi") * lax.axis_size("y"),
    )
    half = swap(rows.reshape(n_core, -1, BLK), "core").sum(0)
    part = swap(half.astype(BF).reshape(n_dom, -1, BLK), DOMAINS).astype(F32).sum(0)
    mine = swap(part.reshape(n_chip, -1, BLK), CHIPS).sum(0)
    part = spread(mine, CHIPS, n_chip).reshape(-1, BLK)
    half = spread(part, DOMAINS, n_dom).reshape(-1, BLK)
    return spread(half, "core", n_core).reshape(-1, BLK)


def algebra(s, g1, hw, hw2, w4, p, i, r):
    eye = jnp.eye(s.shape[0], dtype=F32)
    w1 = s - TAU * g1
    w2 = w1 - TAU * hw
    w3 = w2 - TAU * hw2
    e = TAU * g1.astype(BF).astype(F32)

    def outer(high, middle, low, step):
        b = mm(middle + 0.5 * mm(step, low), step)
        return high + b + b.T

    c1 = outer(w2, w1, s, e)
    m1 = 1.5 * eye - 0.5 * c1
    h2 = mm(mm(m1, outer(hw2, hw, g1, e)), m1)
    s1 = mm(mm(m1, c1), m1)
    w2b = mm(mm(m1, outer(w4, w3, w2, e)), m1)
    e2 = TAU * h2.astype(BF).astype(F32)
    c2 = outer(w2b, s1 - TAU * h2, s1, e2)
    m2 = 1.5 * eye - 0.5 * c2

    q = p.astype(F32) - TAU * i.astype(F32)
    t = q - TAU * r.astype(F32)
    psi1 = mm(m1, q + mm(e, p.astype(F32)))
    wpsi1 = mm(m1, t + mm(e, q))
    psi2 = mm(m2, wpsi1 + mm(e2, psi1))
    return psi2.astype(BF), h2


def per_device(orbitals, potential):
    shape = orbitals.shape
    nb = shape[0]
    n_band = lax.axis_size("zhi") * lax.axis_size("y") * lax.axis_size("core")
    cells = shape[1] * shape[2] * shape[3]
    bands = nb * n_band
    chunk = cells // n_band
    volume = 1.0 / (cells * lax.axis_size("dx") * lax.axis_size("dy"))

    image = hamiltonian(orbitals, potential)
    q = (orbitals.astype(F32) - TAU * image.astype(F32)).astype(BF)
    image_q = hamiltonian(q, potential)

    send = jnp.stack([orbitals, image, image_q]).reshape(3, nb, n_band, chunk // BLK, BLK)
    send = send.transpose(2, 0, 1, 3, 4).reshape(n_band, -1, BLK)
    got = swap(send, BAND).reshape(n_band, 3, nb, chunk // BLK, BLK)
    p, i, r = got.transpose(1, 0, 2, 3, 4).reshape(3, bands, chunk)

    qf = p.astype(F32) - TAU * i.astype(F32)
    qb = qf.astype(BF)
    tb = (qf - TAU * r.astype(F32)).astype(BF)
    grams = [gram(p, p), gram(p, i), gram(qb, i), gram(qb, r), gram(tb, tb)]
    nblk = bands // BLK
    rows = jnp.concatenate([b for g in grams for b in pack(g)], axis=0)
    count = rows.shape[0]
    unit = 8 * n_band * lax.axis_size("dx") * lax.axis_size("dy")
    rows = jnp.pad(rows, ((0, -count % unit), (0, 0)))
    total = reduced(rows)[:count] * volume
    per = nblk * (nblk + 1) // 2
    blocks = total.reshape(NGRAM, per, BLK, BLK)
    mats = [unpack([blocks[g, b] for b in range(per)], nblk) for g in range(NGRAM)]
    psi2, h2 = algebra(*mats, p, i, r)

    back = swap(psi2.reshape(n_band, nb, chunk), BAND)
    new = back.transpose(1, 0, 2).reshape(shape)
    columns = lax.dynamic_slice_in_dim(h2, lax.axis_index(BAND) * nb, nb, 1)
    return new, columns


def solution(mesh):
    n_band, n_dx, n_dy = mesh.devices.shape
    fine = Mesh(
        mesh.devices.reshape(-1, min(8, n_band // 2), 2, n_dx, n_dy), BAND + DOMAINS
    )
    in_specs = (P(BAND, "dx", "dy", None), P("dx", "dy", None))
    out_specs = (P(BAND, "dx", "dy", None), P(None, BAND))
    return jax.shard_map(
        per_device, mesh=fine, in_specs=in_specs, out_specs=out_specs, check_vma=False
    )
```

```python
import functools

import jax
import jax.numpy as jnp
from jax import lax
from jax.experimental import pallas as pl
from jax.experimental.pallas import tpu as pltpu
from jax.sharding import Mesh, PartitionSpec as P

COEFFS = (
    -5369.0 / 1800.0,
    12.0 / 7.0,
    -15.0 / 56.0,
    10.0 / 189.0,
    -1.0 / 112.0,
    2.0 / 1925.0,
    -1.0 / 16632.0,
)
TAU = 0.1
BF = jnp.bfloat16
F32 = jnp.float32
BAND = ("zhi", "yh", "yl", "core")
FAR = ("zhi", "yh")
NEAR = ("dx", "dy", "yl")
BLK = 128
NGRAM = 5


def halo(block):
    count = lax.axis_size("dx")
    up = [(i, (i + 1) % count) for i in range(count)]
    down = [(b, a) for a, b in up]
    other = lax.ppermute(block, "dy", [(0, 1), (1, 0)])
    low = lax.ppermute(block[:, block.shape[1] - 6 :], "dx", up)
    high = lax.ppermute(block[:, :6], "dx", down)
    return other, low, high


def hamiltonian(block, potential):
    other, low, high = halo(block)
    wx, wy = block.shape[1], block.shape[2]
    f = block.astype(F32)
    px = jnp.concatenate([low, block, high], axis=1).astype(F32)
    o = other.astype(F32)
    py = jnp.concatenate([o[:, :, wy - 6 :], f, o[:, :, :6]], axis=2)
    total = 3.0 * COEFFS[0] * f
    for k in range(1, 7):
        along_x = px[:, 6 + k : 6 + k + wx] + px[:, 6 - k : 6 - k + wx]
        along_y = py[:, :, 6 + k : 6 + k + wy] + py[:, :, 6 - k : 6 - k + wy]
        along_z = jnp.roll(f, k, 3) + jnp.roll(f, -k, 3)
        total = total + COEFFS[k] * (along_x + along_y + along_z)
    return (-0.5 * total + potential[None] * f).astype(BF)


def swap(x, axes):
    return lax.all_to_all(x, axes, split_axis=0, concat_axis=0, tiled=True)


def spread(x, axes, size):
    return swap(jnp.broadcast_to(x[None], (size,) + x.shape), axes)


def gram(a, b):
    return lax.dot_general(a, b, (((1,), (1,)), ((), ())), preferred_element_type=F32)


def pairs(nblk):
    return [(r, c) for r in range(nblk) for c in range(r, nblk)]


def pack(g):
    nblk = g.shape[0] // BLK
    return [g[r * BLK : (r + 1) * BLK, c * BLK : (c + 1) * BLK] for r, c in pairs(nblk)]


def reduced(rows):
    n_near, n_far = axes_size(NEAR), axes_size(FAR)
    half = swap(rows.reshape(2, -1, BLK), "core").sum(0)
    part = swap(half.astype(BF).reshape(n_near, -1, BLK), NEAR).astype(F32).sum(0)
    mine = spread(part, FAR, n_far).sum(0)
    half = spread(mine, NEAR, n_near).reshape(-1, BLK)
    return spread(half, "core", 2).reshape(-1, BLK)


def axes_size(axes):
    size = 1
    for axis in axes:
        size *= lax.axis_size(axis)
    return size


def dot(a, b):
    return jnp.dot(a, b, preferred_element_type=F32)


def split(x):
    high = x.astype(BF)
    return high, (x - high.astype(F32)).astype(BF)


def algebra_kernel(volume, rows_ref, p_ref, i_ref, r_ref, psi_ref, h_ref, mats):
    n = p_ref.shape[0]
    nblk = n // BLK
    spots = pairs(nblk)
    for g in range(NGRAM):
        for b, (r, c) in enumerate(spots):
            at = (g * len(spots) + b) * BLK
            tile = rows_ref[at : at + BLK] * volume
            mats[g, r * BLK : (r + 1) * BLK, c * BLK : (c + 1) * BLK] = tile
            if r != c:
                mats[g, c * BLK : (c + 1) * BLK, r * BLK : (r + 1) * BLK] = tile.T
    s, g1, hw, hw2, w4 = (mats[g] for g in range(NGRAM))
    w1 = s - TAU * g1
    w2 = w1 - TAU * hw
    w3 = w2 - TAU * hw2
    row = lax.broadcasted_iota(jnp.int32, (n, n), 0)
    col = lax.broadcasted_iota(jnp.int32, (n, n), 1)
    diag = jnp.where(row == col, 1.5, 0.0).astype(F32)

    def left(h, x):
        high, low = split(x)
        return dot(h, high) + dot(h, low)

    def right(x, h):
        high, low = split(x)
        return dot(high, h) + dot(low, h)

    def full(a, x):
        high, low = split(x)
        return dot(a[0], high) + dot(a[0], low) + dot(a[1], high)

    def outer(high, middle, low, h):
        b = TAU * right(middle + (0.5 * TAU) * left(h, low), h)
        return high + b + b.T

    h = g1.astype(BF)
    c1 = outer(w2, w1, s, h)
    m1 = split(diag - 0.5 * c1)

    def both(x):
        return full(m1, full(m1, x).T)

    h2 = both(outer(hw2, hw, g1, h))
    h_ref[...] = h2
    s1 = both(c1)
    w2b = both(outer(w4, w3, w2, h))
    hh = h2.astype(BF)
    m2 = split(diag - 0.5 * outer(w2b, s1 - TAU * h2, s1, hh))

    p, i = p_ref[...], i_ref[...]
    hp = TAU * dot(h, p)
    hq = hp - (TAU * TAU) * dot(h, i)
    q = p.astype(F32) - TAU * i.astype(F32)
    t = q - TAU * r_ref[...].astype(F32)
    psi1 = full(m1, q + hp)
    wpsi1 = full(m1, t + hq)
    psi_ref[...] = full(m2, wpsi1 + TAU * left(hh, psi1)).astype(BF)


def algebra(rows, p, i, r, volume):
    n, chunk = p.shape
    return pl.pallas_call(
        functools.partial(algebra_kernel, volume),
        out_shape=(
            jax.ShapeDtypeStruct((n, chunk), BF),
            jax.ShapeDtypeStruct((n, n), F32),
        ),
        in_specs=[pl.BlockSpec(memory_space=pltpu.VMEM)] * 4,
        out_specs=(pl.BlockSpec(memory_space=pltpu.VMEM),) * 2,
        scratch_shapes=[pltpu.VMEM((NGRAM, n, n), F32)],
        compiler_params=pltpu.CompilerParams(vmem_limit_bytes=48 * 1024 * 1024),
    )(rows, p, i, r)


def per_device(orbitals, potential):
    shape = orbitals.shape
    nb = shape[0]
    n_band = axes_size(BAND)
    cells = shape[1] * shape[2] * shape[3]
    bands = nb * n_band
    chunk = cells // n_band
    volume = 1.0 / (cells * lax.axis_size("dx") * lax.axis_size("dy"))

    image = hamiltonian(orbitals, potential)
    q = (orbitals.astype(F32) - TAU * image.astype(F32)).astype(BF)
    image_q = hamiltonian(q, potential)

    send = jnp.stack([orbitals, image, image_q]).reshape(3, nb, n_band, chunk // BLK, BLK)
    send = send.transpose(2, 0, 1, 3, 4).reshape(n_band, -1, BLK)
    got = swap(send, BAND).reshape(n_band, 3, nb, chunk // BLK, BLK)
    p, i, r = got.transpose(1, 0, 2, 3, 4).reshape(3, bands, chunk)

    qf = p.astype(F32) - TAU * i.astype(F32)
    qb = qf.astype(BF)
    tb = (qf - TAU * r.astype(F32)).astype(BF)
    grams = [gram(p, p), gram(p, i), gram(qb, i), gram(qb, r), gram(tb, tb)]
    rows = jnp.concatenate([b for g in grams for b in pack(g)], axis=0)
    unit = 8 * n_band * lax.axis_size("dx") * lax.axis_size("dy")
    rows = jnp.pad(rows, ((0, -rows.shape[0] % unit), (0, 0)))
    psi2, h2 = algebra(reduced(rows), p, i, r, volume)

    back = swap(psi2.reshape(n_band, nb, chunk), BAND)
    new = back.transpose(1, 0, 2).reshape(shape)
    columns = lax.dynamic_slice_in_dim(h2, lax.axis_index(BAND) * nb, nb, 1)
    return new, columns


def solution(mesh):
    n_band, n_dx, n_dy = mesh.devices.shape
    near = min(4, n_band // 2)
    far = min(2, n_band // 2 // near)
    fine = Mesh(mesh.devices.reshape(-1, far, near, 2, n_dx, n_dy), BAND + ("dx", "dy"))
    in_specs = (P(BAND, "dx", "dy", None), P("dx", "dy", None))
    out_specs = (P(BAND, "dx", "dy", None), P(None, BAND))
    return jax.shard_map(
        per_device, mesh=fine, in_specs=in_specs, out_specs=out_specs, check_vma=False
    )
```

```python
import functools

import jax
import jax.numpy as jnp
import ml_dtypes
import numpy as np
from jax import lax
from jax.experimental import pallas as pl
from jax.experimental.pallas import tpu as pltpu
from jax.sharding import Mesh, PartitionSpec as P

COEFFS = (
    -5369.0 / 1800.0,
    12.0 / 7.0,
    -15.0 / 56.0,
    10.0 / 189.0,
    -1.0 / 112.0,
    2.0 / 1925.0,
    -1.0 / 16632.0,
)
TAU = 0.1
BF = jnp.bfloat16
F32 = jnp.float32
BAND = ("zhi", "yh", "yl", "core")
FAR = ("zhi", "yh")
NEAR = ("dx", "dy", "yl")
BLK = 128
NGRAM = 5


def parts(matrix):
    high = matrix.astype(np.float32).astype(ml_dtypes.bfloat16)
    return high, (matrix - high.astype(np.float64)).astype(np.float32).astype(ml_dtypes.bfloat16)


def plane_matrix(out_rows, in_rows, wy):
    where = {row: k for k, row in enumerate(in_rows)}
    matrix = np.zeros((len(out_rows), len(in_rows)))
    for k, (side, x, y) in enumerate(out_rows):
        matrix[k, where[side, x, y]] += -1.5 * COEFFS[0]
        for offset in range(1, 7):
            for shift in (offset, -offset):
                matrix[k, where[side, x + shift, y]] += -0.5 * COEFFS[offset]
                at = (side * wy + y + shift) % (2 * wy)
                matrix[k, where[at // wy, x, at % wy]] += -0.5 * COEFFS[offset]
    return matrix


def line_matrix(length):
    matrix = np.zeros((length, length))
    at = np.arange(length)
    for offset in range(1, 7):
        for shift in (offset, -offset):
            matrix[at, (at + shift) % length] += -0.5 * COEFFS[offset]
    return np.kron(np.eye(2), matrix)


def slab(side, first, last, wy):
    return [(side, x, y) for x in range(first, last) for y in range(wy)]


def pack_kernel(p_ref, v_ref, own_ref, last_ref, first_ref, clast_ref, cfirst_ref):
    nb, rows, _ = p_ref.shape
    wide, narrow = last_ref.shape[1], clast_ref.shape[1]
    v = v_ref[...]
    high = v.astype(BF)
    low = (v - high.astype(F32)).astype(BF)
    own_ref[:nb] = p_ref[...]
    own_ref[nb] = high
    own_ref[nb + 1] = low
    last_ref[:nb] = p_ref[:, rows - wide :]
    last_ref[nb] = high[rows - wide :]
    last_ref[nb + 1] = low[rows - wide :]
    first_ref[:nb] = p_ref[:, :wide]
    first_ref[nb] = high[:wide]
    first_ref[nb + 1] = low[:wide]
    clast_ref[...] = p_ref[:, rows - narrow :]
    cfirst_ref[...] = p_ref[:, :narrow]


def stencil_kernel(
    p_ref, v_ref, other_ref, lo_ref, hi_ref, clo_ref, chi_ref,
    a1h_ref, a1l_ref, a2h_ref, a2l_ref, zh_ref, zl_ref, i_ref, r_ref, field,
):
    nb, rows, _ = p_ref.shape
    wide, narrow = lo_ref.shape[1], clo_ref.shape[1]

    def around(low, high, other):
        return jnp.concatenate([low[wide - narrow :], high[:narrow], other], axis=0).astype(F32)

    v = around(lo_ref[nb], hi_ref[nb], other_ref[nb])
    v = v + around(lo_ref[nb + 1], hi_ref[nb + 1], other_ref[nb + 1])
    v = jnp.concatenate([v_ref[...], v], axis=0)
    v = jnp.concatenate([v, v], axis=1)
    for b in range(0, nb, 2):
        at = 0
        for ref in (p_ref, lo_ref, hi_ref, other_ref, clo_ref, chi_ref):
            size = ref.shape[1]
            field[at : at + size, :BLK] = ref[b]
            field[at : at + size, BLK:] = ref[b + 1]
            at += size
        f = field[...]
        centre = jnp.concatenate(
            [
                f[:rows],
                f[rows + wide - narrow : rows + wide],
                f[rows + wide : rows + wide + narrow],
                f[rows + 2 * wide : 2 * rows + 2 * wide],
            ],
            axis=0,
        )
        image = dot(a1h_ref[...], f) + dot(a1l_ref[...], f)
        image = image + dot(centre, zh_ref[...]) + dot(centre, zl_ref[...])
        centre = centre.astype(F32)
        image = (image + v * centre).astype(BF)
        q = (centre - TAU * image.astype(F32)).astype(BF)
        own = q[:rows]
        second = dot(a2h_ref[...], q) + dot(a2l_ref[...], q)
        second = second + dot(own, zh_ref[...]) + dot(own, zl_ref[...])
        second = (second + v[:rows] * own.astype(F32)).astype(BF)
        i_ref[b] = image[:rows, :BLK]
        i_ref[b + 1] = image[:rows, BLK:]
        r_ref[b] = second[:, :BLK]
        r_ref[b + 1] = second[:, BLK:]


def call(kernel, outs, args, scratch=(), limit=32):
    return pl.pallas_call(
        kernel,
        out_shape=tuple(outs),
        in_specs=[pl.BlockSpec(memory_space=pltpu.VMEM)] * len(args),
        out_specs=(pl.BlockSpec(memory_space=pltpu.VMEM),) * len(outs),
        scratch_shapes=list(scratch),
        compiler_params=pltpu.CompilerParams(vmem_limit_bytes=limit * 1024 * 1024),
    )(*args)


def images(orbitals, potential):
    nb, wx, wy, _ = orbitals.shape
    rows, wide, narrow = wx * wy, 12 * wy, 6 * wy
    p = orbitals.reshape(nb, rows, BLK)
    v = potential.reshape(rows, BLK)

    def shape(count, size):
        return jax.ShapeDtypeStruct((count, size, BLK), BF)

    own, last, first, clast, cfirst = call(
        pack_kernel,
        [shape(nb + 2, rows)] + [shape(nb + 2, wide)] * 2 + [shape(nb, narrow)] * 2,
        (p, v),
    )
    count = lax.axis_size("dx")
    up = [(k, (k + 1) % count) for k in range(count)]
    down = [(b, a) for a, b in up]
    low = lax.ppermute(last, "dx", up)
    high = lax.ppermute(first, "dx", down)
    other = lax.ppermute(own, "dy", [(0, 1), (1, 0)])
    cup = [(2 * a + k, 2 * b + 1 - k) for a, b in up for k in range(2)]
    cdown = [(2 * a + k, 2 * b + 1 - k) for a, b in down for k in range(2)]
    clow = lax.ppermute(clast, ("dx", "dy"), cup)
    chigh = lax.ppermute(cfirst, ("dx", "dy"), cdown)

    whole = (
        slab(0, 0, wx, wy) + slab(0, -12, 0, wy) + slab(0, wx, wx + 12, wy)
        + slab(1, 0, wx, wy) + slab(1, -6, 0, wy) + slab(1, wx, wx + 6, wy)
    )
    middle = (
        slab(0, 0, wx, wy) + slab(0, -6, 0, wy) + slab(0, wx, wx + 6, wy) + slab(1, 0, wx, wy)
    )
    tables = (
        *parts(plane_matrix(middle, whole, wy)),
        *parts(plane_matrix(slab(0, 0, wx, wy), middle, wy)),
        *parts(line_matrix(BLK)),
    )
    return call(
        stencil_kernel,
        [shape(nb, rows)] * 2,
        (p, v, other, low, high, clow, chigh) + tuple(jnp.asarray(t) for t in tables),
        [pltpu.VMEM((len(whole), 2 * BLK), BF)],
    )


def swap(x, axes):
    return lax.all_to_all(x, axes, split_axis=0, concat_axis=0, tiled=True)


def spread(x, axes, size):
    return swap(jnp.broadcast_to(x[None], (size,) + x.shape), axes)


def gram(a, b):
    return lax.dot_general(a, b, (((1,), (1,)), ((), ())), preferred_element_type=F32)


def pairs(nblk):
    return [(r, c) for r in range(nblk) for c in range(r, nblk)]


def pack(g):
    nblk = g.shape[0] // BLK
    return [g[r * BLK : (r + 1) * BLK, c * BLK : (c + 1) * BLK] for r, c in pairs(nblk)]


def reduced(rows):
    n_near, n_far = axes_size(NEAR), axes_size(FAR)
    half = swap(rows.astype(BF).reshape(2, -1, BLK), "core").astype(F32).sum(0)
    part = swap(half.astype(BF).reshape(n_near, -1, BLK), NEAR).astype(F32).sum(0)
    mine = swap(part.reshape(n_far, -1, BLK), FAR).sum(0)
    part = spread(mine, FAR, n_far).reshape(-1, BLK)
    half = spread(part, NEAR, n_near).reshape(-1, BLK)
    return spread(half, "core", 2).reshape(-1, BLK)


def axes_size(axes):
    size = 1
    for axis in axes:
        size *= lax.axis_size(axis)
    return size


def dot(a, b):
    return jnp.dot(a, b, preferred_element_type=F32)


def split(x):
    high = x.astype(BF)
    return high, (x - high.astype(F32)).astype(BF)


def algebra_kernel(volume, rows_ref, p_ref, i_ref, r_ref, psi_ref, h_ref, mats):
    n = p_ref.shape[0]
    nblk = n // BLK
    spots = pairs(nblk)
    for g in range(NGRAM):
        for b, (r, c) in enumerate(spots):
            at = (g * len(spots) + b) * BLK
            tile = rows_ref[at : at + BLK] * volume
            mats[g, r * BLK : (r + 1) * BLK, c * BLK : (c + 1) * BLK] = tile
            if r != c:
                mats[g, c * BLK : (c + 1) * BLK, r * BLK : (r + 1) * BLK] = tile.T
    s, g1, hw, hw2, w4 = (mats[g] for g in range(NGRAM))
    w1 = s - TAU * g1
    w2 = w1 - TAU * hw
    w3 = w2 - TAU * hw2
    row = lax.broadcasted_iota(jnp.int32, (n, n), 0)
    col = lax.broadcasted_iota(jnp.int32, (n, n), 1)
    diag = jnp.where(row == col, 1.5, 0.0).astype(F32)

    def left(h, x):
        high, low = split(x)
        return dot(h, high) + dot(h, low)

    def right(x, h):
        high, low = split(x)
        return dot(high, h) + dot(low, h)

    def full(a, x):
        high, low = split(x)
        return dot(a[0], high) + dot(a[0], low) + dot(a[1], high)

    def outer(high, middle, low, h):
        b = TAU * right(middle + (0.5 * TAU) * left(h, low), h)
        return high + b + b.T

    h = g1.astype(BF)
    c1 = outer(w2, w1, s, h)
    m1 = split(diag - 0.5 * c1)

    def both(x):
        return full(m1, full(m1, x).T)

    h2 = both(outer(hw2, hw, g1, h))
    h_ref[...] = h2
    s1 = both(c1)
    w2b = both(outer(w4, w3, w2, h))
    hh = h2.astype(BF)
    m2 = split(diag - 0.5 * outer(w2b, s1 - TAU * h2, s1, hh))

    p, i = p_ref[...], i_ref[...]
    hp = TAU * dot(h, p)
    hq = hp - (TAU * TAU) * dot(h, i)
    q = p.astype(F32) - TAU * i.astype(F32)
    t = q - TAU * r_ref[...].astype(F32)
    psi1 = full(m1, q + hp)
    wpsi1 = full(m1, t + hq)
    psi_ref[...] = full(m2, wpsi1 + TAU * left(hh, psi1)).astype(BF)


def algebra(rows, p, i, r, volume):
    n, chunk = p.shape
    return call(
        functools.partial(algebra_kernel, volume),
        [jax.ShapeDtypeStruct((n, chunk), BF), jax.ShapeDtypeStruct((n, n), F32)],
        (rows, p, i, r),
        [pltpu.VMEM((NGRAM, n, n), F32)],
        48,
    )


def per_device(orbitals, potential):
    shape = orbitals.shape
    nb = shape[0]
    n_band = axes_size(BAND)
    cells = shape[1] * shape[2] * shape[3]
    bands = nb * n_band
    chunk = cells // n_band
    volume = 1.0 / (cells * lax.axis_size("dx") * lax.axis_size("dy"))

    image, image_q = images(orbitals, potential)

    send = jnp.stack([orbitals.reshape(image.shape), image, image_q]).reshape(3, nb, n_band, chunk // BLK, BLK)
    send = send.transpose(2, 0, 1, 3, 4).reshape(n_band, -1, BLK)
    got = swap(send, BAND).reshape(n_band, 3, nb, chunk // BLK, BLK)
    p, i, r = got.transpose(1, 0, 2, 3, 4).reshape(3, bands, chunk)

    qf = p.astype(F32) - TAU * i.astype(F32)
    qb = qf.astype(BF)
    tb = (qf - TAU * r.astype(F32)).astype(BF)
    grams = [gram(p, p), gram(p, i), gram(qb, i), gram(qb, r), gram(tb, tb)]
    rows = jnp.concatenate([b for g in grams for b in pack(g)], axis=0)
    unit = 8 * n_band * lax.axis_size("dx") * lax.axis_size("dy")
    rows = jnp.pad(rows, ((0, -rows.shape[0] % unit), (0, 0)))
    psi2, h2 = algebra(reduced(rows), p, i, r, volume)

    back = swap(psi2.reshape(n_band, nb, chunk), BAND)
    new = back.transpose(1, 0, 2).reshape(shape)
    columns = lax.dynamic_slice_in_dim(h2, lax.axis_index(BAND) * nb, nb, 1)
    return new, columns


def solution(mesh):
    n_band, n_dx, n_dy = mesh.devices.shape
    near = min(2, n_band // 2)
    far = min(4, n_band // 2 // near)
    fine = Mesh(mesh.devices.reshape(-1, far, near, 2, n_dx, n_dy), BAND + ("dx", "dy"))
    in_specs = (P(BAND, "dx", "dy", None), P("dx", "dy", None))
    out_specs = (P(BAND, "dx", "dy", None), P(None, BAND))
    return jax.shard_map(
        per_device, mesh=fine, in_specs=in_specs, out_specs=out_specs, check_vma=False
    )
```

```python
import functools

import jax
import jax.numpy as jnp
import ml_dtypes
import numpy as np
from jax import lax
from jax.experimental import pallas as pl
from jax.experimental.pallas import tpu as pltpu
from jax.sharding import Mesh, PartitionSpec as P

COEFFS = (
    -5369.0 / 1800.0,
    12.0 / 7.0,
    -15.0 / 56.0,
    10.0 / 189.0,
    -1.0 / 112.0,
    2.0 / 1925.0,
    -1.0 / 16632.0,
)
TAU = 0.1
BF = jnp.bfloat16
F32 = jnp.float32
BAND = ("zhi", "yh", "yl", "core")
NEAR = ("dx", "dy", "yl")
BLK = 128
NGRAM = 5


def parts(matrix):
    high = matrix.astype(np.float32).astype(ml_dtypes.bfloat16)
    return high, (matrix - high.astype(np.float64)).astype(np.float32).astype(ml_dtypes.bfloat16)


def plane_matrix(out_rows, in_rows, wy):
    where = {row: k for k, row in enumerate(in_rows)}
    matrix = np.zeros((len(out_rows), len(in_rows)))
    for k, (side, x, y) in enumerate(out_rows):
        matrix[k, where[side, x, y]] += -1.5 * COEFFS[0]
        for offset in range(1, 7):
            for shift in (offset, -offset):
                matrix[k, where[side, x + shift, y]] += -0.5 * COEFFS[offset]
                at = (side * wy + y + shift) % (2 * wy)
                matrix[k, where[at // wy, x, at % wy]] += -0.5 * COEFFS[offset]
    return matrix


def line_matrix(length):
    matrix = np.zeros((length, length))
    at = np.arange(length)
    for offset in range(1, 7):
        for shift in (offset, -offset):
            matrix[at, (at + shift) % length] += -0.5 * COEFFS[offset]
    return np.kron(np.eye(2), matrix)


def slab(side, first, last, wy):
    return [(side, x, y) for x in range(first, last) for y in range(wy)]


def pack_kernel(
    p_hbm, v_hbm, own_ref, last_ref, first_ref, clast_ref, cfirst_ref, v_ref, p_ref, sems
):
    copies = [
        pltpu.make_async_copy(p_hbm, p_ref, sems.at[0]),
        pltpu.make_async_copy(v_hbm, v_ref, sems.at[1]),
    ]
    for copy in copies:
        copy.start()
    for copy in copies:
        copy.wait()
    nb, rows, _ = p_ref.shape
    wide, narrow = last_ref.shape[1], clast_ref.shape[1]
    v = v_ref[...].astype(BF)
    own_ref[:nb] = p_ref[...]
    own_ref[nb] = v
    last_ref[:nb] = p_ref[:, rows - wide :]
    last_ref[nb] = v[rows - wide :]
    first_ref[:nb] = p_ref[:, :wide]
    first_ref[nb] = v[:wide]
    clast_ref[...] = p_ref[:, rows - narrow :]
    cfirst_ref[...] = p_ref[:, :narrow]


def stencil_kernel(
    p_ref, v_ref, other_ref, lo_ref, hi_ref, clo_ref, chi_ref,
    a1h, a1l, a2h, a2l, zh, zl, i_ref, r_ref, field,
    a1h_ref, a1l_ref, a2h_ref, a2l_ref, zh_ref, zl_ref, sems,
):
    tables = ((a1h, a1h_ref), (a1l, a1l_ref), (zh, zh_ref), (zl, zl_ref), (a2h, a2h_ref), (a2l, a2l_ref))
    copies = [pltpu.make_async_copy(a, b, sems.at[k]) for k, (a, b) in enumerate(tables)]
    for copy in copies:
        copy.start()
    nb, rows, _ = i_ref.shape
    wide, narrow = lo_ref.shape[1], clo_ref.shape[1]

    def around(low, high, other):
        return jnp.concatenate([low[wide - narrow :], high[:narrow], other], axis=0).astype(F32)

    v = jnp.concatenate([v_ref[...], around(lo_ref[nb], hi_ref[nb], other_ref[nb])], axis=0)
    v = jnp.concatenate([v, v], axis=1)
    for copy in copies:
        copy.wait()
    for b in range(0, nb, 2):
        at = 0
        for ref in (p_ref, lo_ref, hi_ref, other_ref, clo_ref, chi_ref):
            size = ref.shape[1]
            field[at : at + size, :BLK] = ref[b]
            field[at : at + size, BLK:] = ref[b + 1]
            at += size
        f = field[...]
        centre = jnp.concatenate(
            [
                f[:rows],
                f[rows + wide - narrow : rows + wide],
                f[rows + wide : rows + wide + narrow],
                f[rows + 2 * wide : 2 * rows + 2 * wide],
            ],
            axis=0,
        )
        image = dot(a1h_ref[...], f) + dot(a1l_ref[...], f)
        image = image + dot(centre, zh_ref[...]) + dot(centre, zl_ref[...])
        centre = centre.astype(F32)
        image = (image + v * centre).astype(BF)
        q = (centre - TAU * image.astype(F32)).astype(BF)
        own = q[:rows]
        second = dot(a2h_ref[...], q) + dot(a2l_ref[...], q)
        second = second + dot(own, zh_ref[...]) + dot(own, zl_ref[...])
        second = (second + v[:rows] * own.astype(F32)).astype(BF)
        i_ref[b] = image[:rows, :BLK]
        i_ref[b + 1] = image[:rows, BLK:]
        r_ref[b] = second[:, :BLK]
        r_ref[b + 1] = second[:, BLK:]


def call(kernel, outs, args, scratch=(), limit=32, hbm=0):
    specs = [pl.BlockSpec(memory_space=pltpu.VMEM)] * (len(args) - hbm)
    return pl.pallas_call(
        kernel,
        out_shape=tuple(outs),
        in_specs=specs + [pl.BlockSpec(memory_space=pl.ANY)] * hbm,
        out_specs=(pl.BlockSpec(memory_space=pltpu.VMEM),) * len(outs),
        scratch_shapes=list(scratch),
        compiler_params=pltpu.CompilerParams(vmem_limit_bytes=limit * 1024 * 1024),
    )(*args)


def images(orbitals, potential):
    nb, wx, wy, _ = orbitals.shape
    rows, wide, narrow = wx * wy, 12 * wy, 6 * wy
    p = orbitals.reshape(nb, rows, BLK)
    v = potential.reshape(rows, BLK)

    def shape(count, size):
        return jax.ShapeDtypeStruct((count, size, BLK), BF)

    own, last, first, clast, cfirst, v = call(
        pack_kernel,
        [shape(nb + 1, rows)] + [shape(nb + 1, wide)] * 2 + [shape(nb, narrow)] * 2
        + [jax.ShapeDtypeStruct((rows, BLK), F32)],
        (p, v),
        [pltpu.VMEM(p.shape, BF), pltpu.SemaphoreType.DMA((2,))],
        hbm=2,
    )
    count = lax.axis_size("dx")
    up = [(k, (k + 1) % count) for k in range(count)]
    down = [(b, a) for a, b in up]
    low = lax.ppermute(last, "dx", up)
    high = lax.ppermute(first, "dx", down)
    other = lax.ppermute(own, "dy", [(0, 1), (1, 0)])
    cup = [(2 * a + k, 2 * b + 1 - k) for a, b in up for k in range(2)]
    cdown = [(2 * a + k, 2 * b + 1 - k) for a, b in down for k in range(2)]
    clow = lax.ppermute(clast, ("dx", "dy"), cup)
    chigh = lax.ppermute(cfirst, ("dx", "dy"), cdown)

    whole = (
        slab(0, 0, wx, wy) + slab(0, -12, 0, wy) + slab(0, wx, wx + 12, wy)
        + slab(1, 0, wx, wy) + slab(1, -6, 0, wy) + slab(1, wx, wx + 6, wy)
    )
    middle = (
        slab(0, 0, wx, wy) + slab(0, -6, 0, wy) + slab(0, wx, wx + 6, wy) + slab(1, 0, wx, wy)
    )
    tables = (
        *parts(plane_matrix(middle, whole, wy)),
        *parts(plane_matrix(slab(0, 0, wx, wy), middle, wy)),
        *parts(line_matrix(BLK)),
    )
    image, image_q = call(
        stencil_kernel,
        [shape(nb, rows)] * 2,
        (own, v, other, low, high, clow, chigh) + tuple(jnp.asarray(t) for t in tables),
        [pltpu.VMEM((len(whole), 2 * BLK), BF)]
        + [pltpu.VMEM(t.shape, BF) for t in tables]
        + [pltpu.SemaphoreType.DMA((len(tables),))],
        hbm=len(tables),
    )
    return own[:nb], image, image_q


def swap(x, axes):
    return lax.all_to_all(x, axes, split_axis=0, concat_axis=0, tiled=True)


def spread(x, axes, size):
    return swap(jnp.broadcast_to(x[None], (size,) + x.shape), axes)


def pairs(nblk):
    return [(r, c) for r in range(nblk) for c in range(r, nblk)]


def tri(n):
    return lax.broadcasted_iota(jnp.int32, (n, n), 0), lax.broadcasted_iota(jnp.int32, (n, n), 1)


def gram_kernel(p_ref, i_ref, r_ref, rows_ref):
    p, i, r = p_ref[...], i_ref[...], r_ref[...]
    n = p.shape[0]
    nblk = n // BLK
    qf = p.astype(F32) - TAU * i.astype(F32)
    q = qf.astype(BF)
    t = (qf - TAU * r.astype(F32)).astype(BF)

    def gram(a, b):
        return lax.dot_general(a, b, (((1,), (1,)), ((), ())), preferred_element_type=F32)

    s, g1, hw, hw2, w4 = gram(p, p), gram(i, p), gram(q, i), gram(r, q), gram(t, t)
    row, col = tri(n)
    at = 0
    for a, b in ((s, g1), (hw, hw2)):
        square = jnp.where(row > col, b, a).astype(BF)
        for c in range(nblk):
            rows_ref[at : at + n] = square[:, c * BLK : (c + 1) * BLK]
            at += n
    row, col = tri(BLK)

    def diagonal(g, k):
        block = g[k * BLK : (k + 1) * BLK, k * BLK : (k + 1) * BLK]
        return jnp.sum(jnp.where(row == col, block, 0.0), axis=0, keepdims=True)

    for k, c in pairs(nblk):
        block = w4[k * BLK : (k + 1) * BLK, c * BLK : (c + 1) * BLK]
        if k == c:
            first, second = diagonal(g1, k), diagonal(hw2, k)
            for at_row, line in (
                (BLK - 4, first), (BLK - 3, pltpu.roll(first, 64, 1)),
                (BLK - 2, second), (BLK - 1, pltpu.roll(second, 64, 1)),
            ):
                block = jnp.where((row == at_row) & (col < 64), line, block)
        rows_ref[at : at + BLK] = block.astype(BF)
        at += BLK


def reduced(rows):
    n_near = axes_size(NEAR)
    half = swap(rows.reshape(2, -1, BLK), "core").astype(F32).sum(0)
    part = swap(half.astype(BF).reshape(n_near, -1, BLK), NEAR).astype(F32).sum(0)
    part = spread(part.astype(BF), "zhi", lax.axis_size("zhi")).astype(F32).sum(0)
    part = spread(part, "yh", lax.axis_size("yh")).sum(0)
    half = spread(part, NEAR, n_near).reshape(-1, BLK)
    return spread(half, "core", 2).reshape(-1, BLK)


def axes_size(axes):
    size = 1
    for axis in axes:
        size *= lax.axis_size(axis)
    return size


def dot(a, b):
    return jnp.dot(a, b, preferred_element_type=F32)


def split(x):
    high = x.astype(BF)
    return high, (x - high.astype(F32)).astype(BF)


def algebra_kernel(volume, rows_ref, p_ref, i_ref, r_ref, psi_ref, h_ref, mats):
    n = p_ref.shape[0]
    nblk = n // BLK
    row, col = tri(BLK)

    def put(g, r, c, tile):
        mats[g, r * BLK : (r + 1) * BLK, c * BLK : (c + 1) * BLK] = tile

    at = 2 * nblk * n
    lines = {}
    for r, c in pairs(nblk):
        tile = rows_ref[at : at + BLK] * volume
        at += BLK
        if r == c:
            for g, k in ((1, BLK - 4), (3, BLK - 2)):
                second = pltpu.roll(tile[k + 1 : k + 2], 64, 1)
                lines[g, r] = jnp.where(col[:1] < 64, tile[k : k + 1], second)
            put(4, r, r, jnp.where(row <= col, tile, tile.T))
        else:
            put(4, r, c, tile)
            put(4, c, r, tile.T)
    for g in (0, 2):
        for r in range(nblk):
            for c in range(nblk):
                at = (g // 2 * nblk + c) * n + r * BLK
                tile = rows_ref[at : at + BLK] * volume
                flip = tile.T
                if r == c:
                    put(g, r, r, jnp.where(row <= col, tile, flip))
                    other = jnp.where(row >= col, tile, flip)
                    put(g + 1, r, r, jnp.where(row == col, lines[g + 1, r], other))
                else:
                    to = g if r < c else g + 1
                    put(to, r, c, tile)
                    put(to, c, r, flip)
    s, g1, hw, hw2, w4 = (mats[g] for g in range(NGRAM))
    w1 = s - TAU * g1
    w2 = w1 - TAU * hw
    w3 = w2 - TAU * hw2
    row, col = tri(n)
    diag = jnp.where(row == col, 1.5, 0.0).astype(F32)

    def left(h, x):
        high, low = split(x)
        return dot(h, high) + dot(h, low)

    def right(x, h):
        high, low = split(x)
        return dot(high, h) + dot(low, h)

    def full(a, x):
        high, low = split(x)
        return dot(a[0], high) + dot(a[0], low) + dot(a[1], high)

    def outer(high, middle, low, h):
        b = TAU * right(middle + (0.5 * TAU) * left(h, low), h)
        return high + b + b.T

    h = g1.astype(BF)
    c1 = outer(w2, w1, s, h)
    m1 = split(diag - 0.5 * c1)

    def both(x):
        return full(m1, full(m1, x).T)

    h2 = both(outer(hw2, hw, g1, h))
    h_ref[...] = h2
    s1 = both(c1)
    w2b = both(outer(w4, w3, w2, h))
    hh = h2.astype(BF)
    m2 = split(diag - 0.5 * outer(w2b, s1 - TAU * h2, s1, hh))

    p, i = p_ref[...], i_ref[...]
    hp = TAU * dot(h, p)
    hq = hp - (TAU * TAU) * dot(h, i)
    q = p.astype(F32) - TAU * i.astype(F32)
    t = q - TAU * r_ref[...].astype(F32)
    psi1 = full(m1, q + hp)
    wpsi1 = full(m1, t + hq)
    psi_ref[...] = full(m2, wpsi1 + TAU * left(hh, psi1)).astype(BF)


def algebra(rows, p, i, r, volume):
    n, chunk = p.shape
    return call(
        functools.partial(algebra_kernel, volume),
        [jax.ShapeDtypeStruct((n, chunk), BF), jax.ShapeDtypeStruct((n, n), F32)],
        (rows, p, i, r),
        [pltpu.VMEM((NGRAM, n, n), F32)],
        48,
    )


def per_device(orbitals, potential):
    shape = orbitals.shape
    nb = shape[0]
    n_band = axes_size(BAND)
    cells = shape[1] * shape[2] * shape[3]
    bands = nb * n_band
    chunk = cells // n_band
    volume = 1.0 / (cells * lax.axis_size("dx") * lax.axis_size("dy"))

    psi, image, image_q = images(orbitals, potential)

    send = jnp.stack([psi, image, image_q]).reshape(3, nb, n_band, chunk // BLK, BLK)
    send = send.transpose(2, 0, 1, 3, 4).reshape(n_band, -1, BLK)
    got = swap(send, BAND).reshape(n_band, 3, nb, chunk // BLK, BLK)
    p, i, r = got.transpose(1, 0, 2, 3, 4).reshape(3, bands, chunk)

    count = bands // BLK * 2 * bands + len(pairs(bands // BLK)) * BLK
    (rows,) = call(gram_kernel, [jax.ShapeDtypeStruct((count, BLK), BF)], (p, i, r))
    psi2, h2 = algebra(reduced(rows), p, i, r, volume)

    back = swap(psi2.reshape(n_band, nb, chunk), BAND)
    new = back.transpose(1, 0, 2).reshape(shape)
    columns = lax.dynamic_slice_in_dim(h2, lax.axis_index(BAND) * nb, nb, 1)
    return new, columns


def solution(mesh):
    n_band, n_dx, n_dy = mesh.devices.shape
    near = min(2, n_band // 2)
    far = min(4, n_band // 2 // near)
    fine = Mesh(mesh.devices.reshape(-1, far, near, 2, n_dx, n_dy), BAND + ("dx", "dy"))
    in_specs = (P(BAND, "dx", "dy", None), P("dx", "dy", None))
    out_specs = (P(BAND, "dx", "dy", None), P(None, BAND))
    return jax.shard_map(
        per_device, mesh=fine, in_specs=in_specs, out_specs=out_specs, check_vma=False
    )
```

```python
import functools

import jax
import jax.numpy as jnp
import ml_dtypes
import numpy as np
from jax import lax
from jax.experimental import pallas as pl
from jax.experimental.pallas import tpu as pltpu
from jax.sharding import Mesh, PartitionSpec as P

COEFFS = (
    -5369.0 / 1800.0,
    12.0 / 7.0,
    -15.0 / 56.0,
    10.0 / 189.0,
    -1.0 / 112.0,
    2.0 / 1925.0,
    -1.0 / 16632.0,
)
TAU = 0.1
BF = jnp.bfloat16
F32 = jnp.float32
BAND = ("zhi", "yh", "yl", "core")
NEAR = ("dx", "dy", "yl")
BLK = 128
NGRAM = 5


def parts(matrix):
    high = matrix.astype(np.float32).astype(ml_dtypes.bfloat16)
    return high, (matrix - high.astype(np.float64)).astype(np.float32).astype(ml_dtypes.bfloat16)


def plane_matrix(out_rows, in_rows, wy):
    where = {row: k for k, row in enumerate(in_rows)}
    matrix = np.zeros((len(out_rows), len(in_rows)))
    for k, (side, x, y) in enumerate(out_rows):
        matrix[k, where[side, x, y]] += -1.5 * COEFFS[0]
        for offset in range(1, 7):
            for shift in (offset, -offset):
                matrix[k, where[side, x + shift, y]] += -0.5 * COEFFS[offset]
                at = (side * wy + y + shift) % (2 * wy)
                matrix[k, where[at // wy, x, at % wy]] += -0.5 * COEFFS[offset]
    return matrix


def line_matrix(length):
    matrix = np.zeros((length, length))
    at = np.arange(length)
    for offset in range(1, 7):
        for shift in (offset, -offset):
            matrix[at, (at + shift) % length] += -0.5 * COEFFS[offset]
    return matrix


def slab(side, first, last, wy):
    return [(side, x, y) for x in range(first, last) for y in range(wy)]


def pack_kernel(p_ref, v_ref, own_ref, last_ref, first_ref, clast_ref, cfirst_ref):
    nb, rows, _ = p_ref.shape
    wide, narrow = last_ref.shape[1], clast_ref.shape[1]
    v = v_ref[...].astype(BF)
    own_ref[:nb] = p_ref[...]
    own_ref[nb] = v
    last_ref[:nb] = p_ref[:, rows - wide :]
    last_ref[nb] = v[rows - wide :]
    first_ref[:nb] = p_ref[:, :wide]
    first_ref[nb] = v[:wide]
    clast_ref[...] = p_ref[:, rows - narrow :]
    cfirst_ref[...] = p_ref[:, :narrow]


def stencil_kernel(
    p_ref, v_ref, other_ref, lo_ref, hi_ref, clo_ref, chi_ref,
    table_ref, i_ref, r_ref, field,
):
    size = field.shape[0]
    middle = p_ref.shape[1] + 2 * clo_ref.shape[1] + other_ref.shape[1]
    last = 2 * middle + i_ref.shape[1]
    end = last + i_ref.shape[1]
    corner = table_ref.shape[1] - BLK
    a1h, a1l = table_ref[:middle, :size], table_ref[middle : 2 * middle, :size]
    a2h, a2l = table_ref[2 * middle : last, :middle], table_ref[last:end, :middle]
    zh = table_ref[2 * middle : 2 * middle + BLK, corner:]
    zl = table_ref[2 * middle + BLK : 2 * middle + 2 * BLK, corner:]

    def along_z(x):
        halves = (x[:, :BLK], x[:, BLK:])
        return jnp.concatenate([dot(h, zh) + dot(h, zl) for h in halves], axis=1)

    nb, rows, _ = i_ref.shape
    wide, narrow = lo_ref.shape[1], clo_ref.shape[1]

    def around(low, high, other):
        return jnp.concatenate([low[wide - narrow :], high[:narrow], other], axis=0).astype(F32)

    v = jnp.concatenate([v_ref[...], around(lo_ref[nb], hi_ref[nb], other_ref[nb])], axis=0)
    v = jnp.concatenate([v, v], axis=1)
    for b in range(0, nb, 2):
        at = 0
        for ref in (p_ref, lo_ref, hi_ref, other_ref, clo_ref, chi_ref):
            size = ref.shape[1]
            field[at : at + size, :BLK] = ref[b]
            field[at : at + size, BLK:] = ref[b + 1]
            at += size
        f = field[...]
        centre = jnp.concatenate(
            [
                f[:rows],
                f[rows + wide - narrow : rows + wide],
                f[rows + wide : rows + wide + narrow],
                f[rows + 2 * wide : 2 * rows + 2 * wide],
            ],
            axis=0,
        )
        image = dot(a1h, f) + dot(a1l, f) + along_z(centre)
        centre = centre.astype(F32)
        image = (image + v * centre).astype(BF)
        q = (centre - TAU * image.astype(F32)).astype(BF)
        own = q[:rows]
        second = dot(a2h, q) + dot(a2l, q) + along_z(own)
        second = (second + v[:rows] * own.astype(F32)).astype(BF)
        i_ref[b] = image[:rows, :BLK]
        i_ref[b + 1] = image[:rows, BLK:]
        r_ref[b] = second[:, :BLK]
        r_ref[b + 1] = second[:, BLK:]


def call(kernel, outs, args, scratch=(), limit=32):
    return pl.pallas_call(
        kernel,
        out_shape=tuple(outs),
        in_specs=[pl.BlockSpec(memory_space=pltpu.VMEM)] * len(args),
        out_specs=(pl.BlockSpec(memory_space=pltpu.VMEM),) * len(outs),
        scratch_shapes=list(scratch),
        compiler_params=pltpu.CompilerParams(vmem_limit_bytes=limit * 1024 * 1024),
    )(*args)


def images(orbitals, potential):
    nb, wx, wy, _ = orbitals.shape
    rows, wide, narrow = wx * wy, 12 * wy, 6 * wy
    p = orbitals.reshape(nb, rows, BLK)
    v = potential.reshape(rows, BLK)

    def shape(count, size):
        return jax.ShapeDtypeStruct((count, size, BLK), BF)

    whole = (
        slab(0, 0, wx, wy) + slab(0, -12, 0, wy) + slab(0, wx, wx + 12, wy)
        + slab(1, 0, wx, wy) + slab(1, -6, 0, wy) + slab(1, wx, wx + 6, wy)
    )
    middle = (
        slab(0, 0, wx, wy) + slab(0, -6, 0, wy) + slab(0, wx, wx + 6, wy) + slab(1, 0, wx, wy)
    )
    big = parts(plane_matrix(middle, whole, wy))
    small = parts(plane_matrix(slab(0, 0, wx, wy), middle, wy))
    line = parts(line_matrix(BLK))
    table = np.zeros((2 * len(middle) + 2 * max(rows, BLK), 5 * BLK), ml_dtypes.bfloat16)
    for k in range(2):
        table[k * len(middle) : (k + 1) * len(middle), : len(whole)] = big[k]
        at = 2 * len(middle) + k * rows
        table[at : at + rows, : len(middle)] = small[k]
        at = 2 * len(middle) + k * BLK
        table[at : at + BLK, -BLK:] = line[k]
    own, last, first, clast, cfirst = call(
        pack_kernel,
        [shape(nb + 1, rows)] + [shape(nb + 1, wide)] * 2 + [shape(nb, narrow)] * 2,
        (p, v),
    )
    count = lax.axis_size("dx")
    up = [(k, (k + 1) % count) for k in range(count)]
    down = [(b, a) for a, b in up]
    low = lax.ppermute(last, "dx", up)
    high = lax.ppermute(first, "dx", down)
    other = lax.ppermute(own, "dy", [(0, 1), (1, 0)])
    cup = [(2 * a + k, 2 * b + 1 - k) for a, b in up for k in range(2)]
    cdown = [(2 * a + k, 2 * b + 1 - k) for a, b in down for k in range(2)]
    clow = lax.ppermute(clast, ("dx", "dy"), cup)
    chigh = lax.ppermute(cfirst, ("dx", "dy"), cdown)

    image, image_q = call(
        stencil_kernel,
        [shape(nb, rows)] * 2,
        (p, v, other, low, high, clow, chigh, jnp.asarray(table)),
        [pltpu.VMEM((len(whole), 2 * BLK), BF)],
    )
    return p, image, image_q


def swap(x, axes):
    return lax.all_to_all(x, axes, split_axis=0, concat_axis=0, tiled=True)


def spread(x, axes, size):
    return swap(jnp.broadcast_to(x[None], (size,) + x.shape), axes)


def pairs(nblk):
    return [(r, c) for r in range(nblk) for c in range(r, nblk)]


def tri(n):
    return lax.broadcasted_iota(jnp.int32, (n, n), 0), lax.broadcasted_iota(jnp.int32, (n, n), 1)


def gram_kernel(p_ref, i_ref, r_ref, rows_ref):
    p, i, r = p_ref[...], i_ref[...], r_ref[...]
    n = p.shape[0]
    nblk = n // BLK
    qf = p.astype(F32) - TAU * i.astype(F32)
    q = qf.astype(BF)
    t = (qf - TAU * r.astype(F32)).astype(BF)

    def gram(a, b):
        return lax.dot_general(a, b, (((1,), (1,)), ((), ())), preferred_element_type=F32)

    s, g1, hw, hw2, w4 = gram(p, p), gram(i, p), gram(q, i), gram(r, q), gram(t, t)
    row, col = tri(n)
    at = 0
    for a, b in ((s, g1), (hw, hw2)):
        square = jnp.where(row > col, b, a).astype(BF)
        for c in range(nblk):
            rows_ref[at : at + n] = square[:, c * BLK : (c + 1) * BLK]
            at += n
    row, col = tri(BLK)

    def diagonal(g, k):
        block = g[k * BLK : (k + 1) * BLK, k * BLK : (k + 1) * BLK]
        return jnp.sum(jnp.where(row == col, block, 0.0), axis=0, keepdims=True)

    for k, c in pairs(nblk):
        block = w4[k * BLK : (k + 1) * BLK, c * BLK : (c + 1) * BLK]
        if k == c:
            first, second = diagonal(g1, k), diagonal(hw2, k)
            for at_row, line in (
                (BLK - 4, first), (BLK - 3, pltpu.roll(first, 64, 1)),
                (BLK - 2, second), (BLK - 1, pltpu.roll(second, 64, 1)),
            ):
                block = jnp.where((row == at_row) & (col < 64), line, block)
        rows_ref[at : at + BLK] = block.astype(BF)
        at += BLK


def reduced(rows):
    n_near = axes_size(NEAR)
    half = swap(rows.reshape(2, -1, BLK), "core").astype(F32).sum(0)
    part = swap(half.astype(BF).reshape(n_near, -1, BLK), NEAR).astype(F32).sum(0)
    part = spread(part.astype(BF), "zhi", lax.axis_size("zhi")).astype(F32).sum(0)
    part = spread(part, "yh", lax.axis_size("yh")).sum(0)
    half = spread(part, NEAR, n_near).reshape(-1, BLK)
    return spread(half, "core", 2).reshape(-1, BLK)


def axes_size(axes):
    size = 1
    for axis in axes:
        size *= lax.axis_size(axis)
    return size


def dot(a, b):
    return jnp.dot(a, b, preferred_element_type=F32)


def split(x):
    high = x.astype(BF)
    return high, (x - high.astype(F32)).astype(BF)


def algebra_kernel(volume, rows_ref, p_ref, i_ref, r_ref, psi_ref, h_ref, mats):
    n = p_ref.shape[0]
    nblk = n // BLK
    row, col = tri(BLK)

    def put(g, r, c, tile):
        mats[g, r * BLK : (r + 1) * BLK, c * BLK : (c + 1) * BLK] = tile

    at = 2 * nblk * n
    lines = {}
    for r, c in pairs(nblk):
        tile = rows_ref[at : at + BLK] * volume
        at += BLK
        if r == c:
            for g, k in ((1, BLK - 4), (3, BLK - 2)):
                second = pltpu.roll(tile[k + 1 : k + 2], 64, 1)
                lines[g, r] = jnp.where(col[:1] < 64, tile[k : k + 1], second)
            put(4, r, r, jnp.where(row <= col, tile, tile.T))
        else:
            put(4, r, c, tile)
            put(4, c, r, tile.T)
    for g in (0, 2):
        for r in range(nblk):
            for c in range(nblk):
                at = (g // 2 * nblk + c) * n + r * BLK
                tile = rows_ref[at : at + BLK] * volume
                flip = tile.T
                if r == c:
                    put(g, r, r, jnp.where(row <= col, tile, flip))
                    other = jnp.where(row >= col, tile, flip)
                    put(g + 1, r, r, jnp.where(row == col, lines[g + 1, r], other))
                else:
                    to = g if r < c else g + 1
                    put(to, r, c, tile)
                    put(to, c, r, flip)
    s, g1, hw, hw2, w4 = (mats[g] for g in range(NGRAM))
    w1 = s - TAU * g1
    w2 = w1 - TAU * hw
    w3 = w2 - TAU * hw2
    row, col = tri(n)
    diag = jnp.where(row == col, 1.5, 0.0).astype(F32)

    def full(a, x):
        high, low = split(x)
        return dot(a[0], high) + dot(a[0], low) + dot(a[1], high)

    def outer(high, middle, low, h):
        b = middle + (0.5 * TAU) * dot(h, low.astype(BF))
        b = TAU * dot(b.astype(BF), h)
        return high + b + b.T

    h = g1.astype(BF)
    c1 = outer(w2, w1, s, h)
    m1 = split(diag - 0.5 * c1)

    def both(x):
        return full(m1, full(m1, x).T)

    def both_rounded(x):
        x = x.astype(BF)
        x = (dot(m1[0], x) + dot(m1[1], x)).T.astype(BF)
        return dot(m1[0], x) + dot(m1[1], x)

    h2 = both(outer(hw2, hw, g1, h))
    h_ref[...] = h2
    s1 = both_rounded(c1)
    w2b = both_rounded(outer(w4, w3, w2, h))
    hh = h2.astype(BF)
    m2 = split(diag - 0.5 * outer(w2b, s1 - TAU * h2, s1, hh))

    p, i = p_ref[...], i_ref[...]
    hp = TAU * dot(h, p)
    hq = hp - (TAU * TAU) * dot(h, i)
    q = p.astype(F32) - TAU * i.astype(F32)
    t = q - TAU * r_ref[...].astype(F32)
    psi1 = full(m1, q + hp)
    wpsi1 = full(m1, t + hq)
    psi_ref[...] = full(m2, wpsi1 + TAU * dot(hh, psi1.astype(BF))).astype(BF)


def algebra(rows, p, i, r, volume):
    n, chunk = p.shape
    return call(
        functools.partial(algebra_kernel, volume),
        [jax.ShapeDtypeStruct((n, chunk), BF), jax.ShapeDtypeStruct((n, n), F32)],
        (rows, p, i, r),
        [pltpu.VMEM((NGRAM, n, n), F32)],
        48,
    )


def per_device(orbitals, potential):
    shape = orbitals.shape
    nb = shape[0]
    n_band = axes_size(BAND)
    cells = shape[1] * shape[2] * shape[3]
    bands = nb * n_band
    chunk = cells // n_band
    volume = 1.0 / (cells * lax.axis_size("dx") * lax.axis_size("dy"))

    psi, image, image_q = images(orbitals, potential)

    send = jnp.stack([psi, image, image_q]).reshape(3, nb, n_band, chunk // BLK, BLK)
    send = send.transpose(2, 0, 1, 3, 4).reshape(n_band, -1, BLK)
    got = swap(send, BAND).reshape(n_band, 3, nb, chunk // BLK, BLK)
    p, i, r = got.transpose(1, 0, 2, 3, 4).reshape(3, bands, chunk)

    count = bands // BLK * 2 * bands + len(pairs(bands // BLK)) * BLK
    (rows,) = call(gram_kernel, [jax.ShapeDtypeStruct((count, BLK), BF)], (p, i, r))
    psi2, h2 = algebra(reduced(rows), p, i, r, volume)

    back = swap(psi2.reshape(n_band, nb, chunk), BAND)
    new = back.transpose(1, 0, 2).reshape(shape)
    columns = lax.dynamic_slice_in_dim(h2, lax.axis_index(BAND) * nb, nb, 1)
    return new, columns


def solution(mesh):
    n_band, n_dx, n_dy = mesh.devices.shape
    near = min(2, n_band // 2)
    far = min(4, n_band // 2 // near)
    fine = Mesh(mesh.devices.reshape(-1, far, near, 2, n_dx, n_dy), BAND + ("dx", "dy"))
    in_specs = (P(BAND, "dx", "dy", None), P("dx", "dy", None))
    out_specs = (P(BAND, "dx", "dy", None), P(None, BAND))
    return jax.shard_map(
        per_device, mesh=fine, in_specs=in_specs, out_specs=out_specs, check_vma=False
    )
```

```python
import functools

import jax
import jax.numpy as jnp
import ml_dtypes
import numpy as np
from jax import lax
from jax.experimental import pallas as pl
from jax.experimental.pallas import tpu as pltpu
from jax.sharding import Mesh, PartitionSpec as P

COEFFS = (
    -5369.0 / 1800.0,
    12.0 / 7.0,
    -15.0 / 56.0,
    10.0 / 189.0,
    -1.0 / 112.0,
    2.0 / 1925.0,
    -1.0 / 16632.0,
)
TAU = 0.1
BF = jnp.bfloat16
F32 = jnp.float32
BAND = ("zhi", "yh", "yl", "core")
NEAR = ("dx", "dy", "yl")
BLK = 128
NGRAM = 5


def parts(matrix):
    high = matrix.astype(np.float32).astype(ml_dtypes.bfloat16)
    return high, (matrix - high.astype(np.float64)).astype(np.float32).astype(ml_dtypes.bfloat16)


def plane_matrix(out_rows, in_rows, wy):
    where = {row: k for k, row in enumerate(in_rows)}
    matrix = np.zeros((len(out_rows), len(in_rows)))
    for k, (side, x, y) in enumerate(out_rows):
        matrix[k, where[side, x, y]] += -1.5 * COEFFS[0]
        for offset in range(1, 7):
            for shift in (offset, -offset):
                matrix[k, where[side, x + shift, y]] += -0.5 * COEFFS[offset]
                at = (side * wy + y + shift) % (2 * wy)
                matrix[k, where[at // wy, x, at % wy]] += -0.5 * COEFFS[offset]
    return matrix


def line_matrix(length):
    matrix = np.zeros((length, length))
    at = np.arange(length)
    for offset in range(1, 7):
        for shift in (offset, -offset):
            matrix[at, (at + shift) % length] += -0.5 * COEFFS[offset]
    return matrix


def slab(side, first, last, wy):
    return [(side, x, y) for x in range(first, last) for y in range(wy)]


def pack_kernel(p_ref, v_ref, own_ref):
    nb = p_ref.shape[0]
    own_ref[:nb] = p_ref[...]
    own_ref[nb] = v_ref[...].astype(BF)


def edge_kernel(wide, own_ref, other_ref, last_ref, first_ref):
    rows = own_ref.shape[1]
    narrow = last_ref.shape[1] - wide
    last_ref[:, :wide] = own_ref[:, rows - wide :]
    last_ref[:, wide:] = other_ref[:, rows - narrow :]
    first_ref[:, :wide] = own_ref[:, :wide]
    first_ref[:, wide:] = other_ref[:, :narrow]


def stencil_kernel(wide, p_ref, v_ref, other_ref, lo_ref, hi_ref, table_ref, out_ref, field):
    size = field.shape[0]
    nb, rows, _ = p_ref.shape
    narrow = lo_ref.shape[1] - wide
    middle = 2 * rows + 2 * narrow
    last = 2 * middle + rows
    end = last + rows
    corner = table_ref.shape[1] - BLK
    a1h, a1l = table_ref[:middle, :size], table_ref[middle : 2 * middle, :size]
    a2h, a2l = table_ref[2 * middle : last, :middle], table_ref[last:end, :middle]
    zh = table_ref[2 * middle : 2 * middle + BLK, corner:]
    zl = table_ref[2 * middle + BLK : 2 * middle + 2 * BLK, corner:]

    def along_z(x):
        halves = (x[:, :BLK], x[:, BLK:])
        return jnp.concatenate([dot(h, zh) + dot(h, zl) for h in halves], axis=1)

    def around(low, high, other):
        return jnp.concatenate([low[wide - narrow : wide], high[:narrow], other], axis=0).astype(F32)

    v = jnp.concatenate([v_ref[...], around(lo_ref[nb], hi_ref[nb], other_ref[nb])], axis=0)
    v = jnp.concatenate([v, v], axis=1)
    chunks = out_ref.shape[1]
    parts_out = rows // chunks
    for b in range(0, nb, 2):
        at = 0
        for ref, first, size in (
            (p_ref, 0, rows), (lo_ref, 0, wide), (hi_ref, 0, wide),
            (other_ref, 0, rows), (lo_ref, wide, narrow), (hi_ref, wide, narrow),
        ):
            field[at : at + size, :BLK] = ref[b, first : first + size]
            field[at : at + size, BLK:] = ref[b + 1, first : first + size]
            at += size
        f = field[...]
        centre = jnp.concatenate(
            [
                f[:rows],
                f[rows + wide - narrow : rows + wide],
                f[rows + wide : rows + wide + narrow],
                f[rows + 2 * wide : 2 * rows + 2 * wide],
            ],
            axis=0,
        )
        image = dot(a1h, f) + dot(a1l, f) + along_z(centre)
        centre = centre.astype(F32)
        image = (image + v * centre).astype(BF)
        q = (centre - TAU * image.astype(F32)).astype(BF)
        own = q[:rows]
        second = dot(a2h, q) + dot(a2l, q) + along_z(own)
        second = (second + v[:rows] * own.astype(F32)).astype(BF)
        for k, x in enumerate((f[:rows], image[:rows], second)):
            for h in range(parts_out):
                for j in range(2):
                    block = x[h * chunks : (h + 1) * chunks, j * BLK : (j + 1) * BLK]
                    out_ref[(k * parts_out + h) * nb + b + j] = block


def call(kernel, outs, args, scratch=(), limit=32):
    return pl.pallas_call(
        kernel,
        out_shape=tuple(outs),
        in_specs=[pl.BlockSpec(memory_space=pltpu.VMEM)] * len(args),
        out_specs=(pl.BlockSpec(memory_space=pltpu.VMEM),) * len(outs),
        scratch_shapes=list(scratch),
        compiler_params=pltpu.CompilerParams(vmem_limit_bytes=limit * 1024 * 1024),
    )(*args)


def images(orbitals, potential, chunks):
    nb, wx, wy, _ = orbitals.shape
    rows, wide, narrow = wx * wy, 12 * wy, 6 * wy
    p = orbitals.reshape(nb, rows, BLK)
    v = potential.reshape(rows, BLK)

    def shape(count, size):
        return jax.ShapeDtypeStruct((count, size, BLK), BF)

    whole = (
        slab(0, 0, wx, wy) + slab(0, -12, 0, wy) + slab(0, wx, wx + 12, wy)
        + slab(1, 0, wx, wy) + slab(1, -6, 0, wy) + slab(1, wx, wx + 6, wy)
    )
    middle = (
        slab(0, 0, wx, wy) + slab(0, -6, 0, wy) + slab(0, wx, wx + 6, wy) + slab(1, 0, wx, wy)
    )
    big = parts(plane_matrix(middle, whole, wy))
    small = parts(plane_matrix(slab(0, 0, wx, wy), middle, wy))
    line = parts(line_matrix(BLK))
    table = np.zeros((2 * len(middle) + 2 * max(rows, BLK), 5 * BLK), ml_dtypes.bfloat16)
    for k in range(2):
        table[k * len(middle) : (k + 1) * len(middle), : len(whole)] = big[k]
        at = 2 * len(middle) + k * rows
        table[at : at + rows, : len(middle)] = small[k]
        at = 2 * len(middle) + k * BLK
        table[at : at + BLK, -BLK:] = line[k]
    (own,) = call(pack_kernel, [shape(nb + 1, rows)], (p, v))
    other = lax.ppermute(own, "dy", [(0, 1), (1, 0)])
    last, first = call(
        functools.partial(edge_kernel, wide), [shape(nb + 1, wide + narrow)] * 2, (own, other)
    )
    count = lax.axis_size("dx")
    up = [(k, (k + 1) % count) for k in range(count)]
    low = lax.ppermute(last, "dx", up)
    high = lax.ppermute(first, "dx", [(b, a) for a, b in up])
    return call(
        functools.partial(stencil_kernel, wide),
        [shape(3 * nb * rows // chunks, chunks)],
        (p, v, other, low, high, jnp.asarray(table)),
        [pltpu.VMEM((len(whole), 2 * BLK), BF)],
    )[0]


def swap(x, axes):
    return lax.all_to_all(x, axes, split_axis=0, concat_axis=0, tiled=True)


def spread(x, axes, size):
    return swap(jnp.broadcast_to(x[None], (size,) + x.shape), axes)


def pairs(nblk):
    return [(r, c) for r in range(nblk) for c in range(r, nblk)]


def tri(n):
    return lax.broadcasted_iota(jnp.int32, (n, n), 0), lax.broadcasted_iota(jnp.int32, (n, n), 1)


def panels(x_ref):
    return [
        jnp.concatenate([x_ref[k, h] for h in range(x_ref.shape[1])], axis=1) for k in range(3)
    ]


def gram_kernel(x_ref, rows_ref):
    p, i, r = panels(x_ref)
    n = p.shape[0]
    nblk = n // BLK
    qf = p.astype(F32) - TAU * i.astype(F32)
    q = qf.astype(BF)
    t = (qf - TAU * r.astype(F32)).astype(BF)

    def gram(a, b):
        return lax.dot_general(a, b, (((1,), (1,)), ((), ())), preferred_element_type=F32)

    s, g1, hw, hw2, w4 = gram(p, p), gram(i, p), gram(q, i), gram(r, q), gram(t, t)
    row, col = tri(n)
    at = 0
    for a, b in ((s, g1), (hw, hw2)):
        square = jnp.where(row > col, b, a).astype(BF)
        for c in range(nblk):
            rows_ref[at : at + n] = square[:, c * BLK : (c + 1) * BLK]
            at += n
    row, col = tri(BLK)

    def diagonal(g, k):
        block = g[k * BLK : (k + 1) * BLK, k * BLK : (k + 1) * BLK]
        return jnp.sum(jnp.where(row == col, block, 0.0), axis=0, keepdims=True)

    for k, c in pairs(nblk):
        block = w4[k * BLK : (k + 1) * BLK, c * BLK : (c + 1) * BLK]
        if k == c:
            first, second = diagonal(g1, k), diagonal(hw2, k)
            for at_row, line in (
                (BLK - 4, first), (BLK - 3, pltpu.roll(first, 64, 1)),
                (BLK - 2, second), (BLK - 1, pltpu.roll(second, 64, 1)),
            ):
                block = jnp.where((row == at_row) & (col < 64), line, block)
        rows_ref[at : at + BLK] = block.astype(BF)
        at += BLK


def reduced(rows):
    n_near = axes_size(NEAR)
    half = swap(rows.reshape(2, -1, BLK), "core").astype(F32).sum(0)
    part = swap(half.astype(BF).reshape(n_near, -1, BLK), NEAR).astype(F32).sum(0)
    part = spread(part.astype(BF), "zhi", lax.axis_size("zhi")).astype(F32).sum(0)
    part = spread(part, "yh", lax.axis_size("yh")).sum(0)
    half = spread(part, NEAR, n_near).reshape(-1, BLK)
    return spread(half, "core", 2).reshape(-1, BLK)


def axes_size(axes):
    size = 1
    for axis in axes:
        size *= lax.axis_size(axis)
    return size


def dot(a, b):
    return jnp.dot(a, b, preferred_element_type=F32)


def split(x):
    high = x.astype(BF)
    return high, (x - high.astype(F32)).astype(BF)


def algebra_kernel(volume, rows_ref, x_ref, psi_ref, h_ref, mats):
    n = x_ref.shape[2]
    nblk = n // BLK
    row, col = tri(BLK)

    def put(g, r, c, tile):
        mats[g, r * BLK : (r + 1) * BLK, c * BLK : (c + 1) * BLK] = tile

    at = 2 * nblk * n
    lines = {}
    for r, c in pairs(nblk):
        tile = rows_ref[at : at + BLK] * volume
        at += BLK
        if r == c:
            for g, k in ((1, BLK - 4), (3, BLK - 2)):
                second = pltpu.roll(tile[k + 1 : k + 2], 64, 1)
                lines[g, r] = jnp.where(col[:1] < 64, tile[k : k + 1], second)
            put(4, r, r, jnp.where(row <= col, tile, tile.T))
        else:
            put(4, r, c, tile)
            put(4, c, r, tile.T)
    for g in (0, 2):
        for r in range(nblk):
            for c in range(nblk):
                at = (g // 2 * nblk + c) * n + r * BLK
                tile = rows_ref[at : at + BLK] * volume
                flip = tile.T
                if r == c:
                    put(g, r, r, jnp.where(row <= col, tile, flip))
                    other = jnp.where(row >= col, tile, flip)
                    put(g + 1, r, r, jnp.where(row == col, lines[g + 1, r], other))
                else:
                    to = g if r < c else g + 1
                    put(to, r, c, tile)
                    put(to, c, r, flip)
    s, g1, hw, hw2, w4 = (mats[g] for g in range(NGRAM))
    w1 = s - TAU * g1
    w2 = w1 - TAU * hw
    w3 = w2 - TAU * hw2
    row, col = tri(n)
    diag = jnp.where(row == col, 1.5, 0.0).astype(F32)

    def full(a, x):
        high, low = split(x)
        return dot(a[0], high) + dot(a[0], low) + dot(a[1], high)

    def outer(high, middle, low, h):
        b = middle + (0.5 * TAU) * dot(h, low.astype(BF))
        b = TAU * dot(b.astype(BF), h)
        return high + b + b.T

    h = g1.astype(BF)
    c1 = outer(w2, w1, s, h)
    m1 = split(diag - 0.5 * c1)

    def both(x):
        return full(m1, full(m1, x).T)

    def both_rounded(x):
        x = x.astype(BF)
        x = (dot(m1[0], x) + dot(m1[1], x)).T.astype(BF)
        return dot(m1[0], x) + dot(m1[1], x)

    h2 = both(outer(hw2, hw, g1, h))
    h_ref[...] = h2
    s1 = both_rounded(c1)
    w2b = both_rounded(outer(w4, w3, w2, h))
    hh = h2.astype(BF)
    m2 = split(diag - 0.5 * outer(w2b, s1 - TAU * h2, s1, hh))

    p, i, r = panels(x_ref)
    hp = TAU * dot(h, p)
    hq = hp - (TAU * TAU) * dot(h, i)
    q = p.astype(F32) - TAU * i.astype(F32)
    t = q - TAU * r.astype(F32)
    psi1 = full(m1, q + hp)
    wpsi1 = full(m1, t + hq)
    psi2 = full(m2, wpsi1 + TAU * dot(hh, psi1.astype(BF))).astype(BF)
    group = psi_ref.shape[1]
    nh = x_ref.shape[1]
    for b in range(n // group):
        for h in range(nh):
            psi_ref[b * nh + h] = psi2[b * group : (b + 1) * group, h * BLK : (h + 1) * BLK]


def algebra(rows, x, volume, n_band):
    n = x.shape[2]
    count = n // n_band * x.shape[1]
    return call(
        functools.partial(algebra_kernel, volume),
        [jax.ShapeDtypeStruct((count, n_band, BLK), BF), jax.ShapeDtypeStruct((n, n), F32)],
        (rows, x),
        [pltpu.VMEM((NGRAM, n, n), F32)],
        48,
    )


def per_device(orbitals, potential):
    shape = orbitals.shape
    nb = shape[0]
    n_band = axes_size(BAND)
    cells = shape[1] * shape[2] * shape[3]
    bands = nb * n_band
    chunk = cells // n_band
    volume = 1.0 / (cells * lax.axis_size("dx") * lax.axis_size("dy"))

    send = images(orbitals, potential, n_band).transpose(1, 0, 2)
    got = swap(send, BAND).transpose(1, 0, 2)
    x = got.reshape(3, chunk // BLK, bands, BLK)

    count = bands // BLK * 2 * bands + len(pairs(bands // BLK)) * BLK
    (rows,) = call(gram_kernel, [jax.ShapeDtypeStruct((count, BLK), BF)], (x,))
    psi2, h2 = algebra(reduced(rows), x, volume, n_band)

    back = swap(psi2.transpose(1, 0, 2), BAND).transpose(1, 0, 2)
    mine = lax.dynamic_index_in_dim(h2.reshape(nb, n_band, bands), lax.axis_index(BAND), 1, False)
    columns = mine.reshape(nb, nb, n_band).transpose(2, 1, 0).reshape(bands, nb)
    return back.reshape(shape), columns


def solution(mesh):
    n_band, n_dx, n_dy = mesh.devices.shape
    near = min(2, n_band // 2)
    far = min(4, n_band // 2 // near)
    fine = Mesh(mesh.devices.reshape(-1, far, near, 2, n_dx, n_dy), BAND + ("dx", "dy"))
    in_specs = (P(BAND, "dx", "dy", None), P("dx", "dy", None))
    out_specs = (P(BAND, "dx", "dy", None), P(None, BAND))
    return jax.shard_map(
        per_device, mesh=fine, in_specs=in_specs, out_specs=out_specs, check_vma=False
    )
```

```python
import functools

import jax
import jax.numpy as jnp
import ml_dtypes
import numpy as np
from jax import lax
from jax.experimental import pallas as pl
from jax.experimental.pallas import tpu as pltpu
from jax.sharding import Mesh, PartitionSpec as P

COEFFS = (
    -5369.0 / 1800.0,
    12.0 / 7.0,
    -15.0 / 56.0,
    10.0 / 189.0,
    -1.0 / 112.0,
    2.0 / 1925.0,
    -1.0 / 16632.0,
)
TAU = 0.1
BF = jnp.bfloat16
F32 = jnp.float32
BAND = ("zhi", "yh", "yl", "core")
NEAR = ("dx", "dy", "yl")
BLK = 128
NGRAM = 5


def parts(matrix):
    high = matrix.astype(np.float32).astype(ml_dtypes.bfloat16)
    return high, (matrix - high.astype(np.float64)).astype(np.float32).astype(ml_dtypes.bfloat16)


def plane_matrix(out_rows, in_rows, wy):
    where = {row: k for k, row in enumerate(in_rows)}
    matrix = np.zeros((len(out_rows), len(in_rows)))
    for k, (side, x, y) in enumerate(out_rows):
        matrix[k, where[side, x, y]] += -1.5 * COEFFS[0]
        for offset in range(1, 7):
            for shift in (offset, -offset):
                matrix[k, where[side, x + shift, y]] += -0.5 * COEFFS[offset]
                at = (side * wy + y + shift) % (2 * wy)
                matrix[k, where[at // wy, x, at % wy]] += -0.5 * COEFFS[offset]
    return matrix


def line_matrix(length):
    matrix = np.zeros((length, length))
    at = np.arange(length)
    for offset in range(1, 7):
        for shift in (offset, -offset):
            matrix[at, (at + shift) % length] += -0.5 * COEFFS[offset]
    return matrix


def slab(side, first, last, wy):
    return [(side, x, y) for x in range(first, last) for y in range(wy)]


def hold_kernel(table_ref, held_ref):
    held_ref[...] = table_ref[...]


def edge_kernel(wide, p_ref, v_ref, other_ref, other_v_ref, last_ref, first_ref):
    nb, rows, _ = p_ref.shape
    narrow = last_ref.shape[1] - wide
    last_ref[:nb, :wide] = p_ref[:, rows - wide :]
    first_ref[:nb, :wide] = p_ref[:, :wide]
    last_ref[:nb, wide:] = other_ref[:, rows - narrow :]
    first_ref[:nb, wide:] = other_ref[:, :narrow]
    last_ref[nb, :wide] = v_ref[rows - wide :]
    first_ref[nb, :wide] = v_ref[:wide]
    last_ref[nb, wide:] = other_v_ref[rows - narrow :]
    first_ref[nb, wide:] = other_v_ref[:narrow]


def stencil_kernel(
    wide, p_ref, v_ref, other_ref, other_v_ref, lo_ref, hi_ref, table_ref, out_ref, field
):
    size = field.shape[0]
    nb, rows, _ = p_ref.shape
    narrow = lo_ref.shape[1] - wide
    middle = 2 * rows + 2 * narrow
    last = 2 * middle + rows
    end = last + rows
    corner = table_ref.shape[1] - BLK
    a1h, a1l = table_ref[:middle, :size], table_ref[middle : 2 * middle, :size]
    a2h, a2l = table_ref[2 * middle : last, :middle], table_ref[last:end, :middle]
    zh = table_ref[2 * middle : 2 * middle + BLK, corner:]
    zl = table_ref[2 * middle + BLK : 2 * middle + 2 * BLK, corner:]

    def along_z(x):
        halves = (x[:, :BLK], x[:, BLK:])
        return jnp.concatenate([dot(h, zh) + dot(h, zl) for h in halves], axis=1)

    def around(low, high, other):
        return jnp.concatenate([low[wide - narrow : wide], high[:narrow], other], axis=0).astype(F32)

    v = jnp.concatenate([v_ref[...], around(lo_ref[nb], hi_ref[nb], other_v_ref[...])], axis=0)
    v = jnp.concatenate([v, v], axis=1)
    chunks = out_ref.shape[1]
    parts_out = rows // chunks
    for b in range(0, nb, 2):
        at = 0
        for ref, first, size in (
            (p_ref, 0, rows), (lo_ref, 0, wide), (hi_ref, 0, wide),
            (other_ref, 0, rows), (lo_ref, wide, narrow), (hi_ref, wide, narrow),
        ):
            field[at : at + size, :BLK] = ref[b, first : first + size]
            field[at : at + size, BLK:] = ref[b + 1, first : first + size]
            at += size
        f = field[...]
        centre = jnp.concatenate(
            [
                f[:rows],
                f[rows + wide - narrow : rows + wide],
                f[rows + wide : rows + wide + narrow],
                f[rows + 2 * wide : 2 * rows + 2 * wide],
            ],
            axis=0,
        )
        image = dot(a1h, f) + dot(a1l, f) + along_z(centre)
        centre = centre.astype(F32)
        image = (image + v * centre).astype(BF)
        q = (centre - TAU * image.astype(F32)).astype(BF)
        own = q[:rows]
        second = dot(a2h, q) + dot(a2l, q) + along_z(own)
        second = (second + v[:rows] * own.astype(F32)).astype(BF)
        for k, x in enumerate((f[:rows], image[:rows], second)):
            for h in range(parts_out):
                for j in range(2):
                    block = x[h * chunks : (h + 1) * chunks, j * BLK : (j + 1) * BLK]
                    out_ref[(k * parts_out + h) * nb + b + j] = block


def call(kernel, outs, args, scratch=(), limit=32, cost=None):
    return pl.pallas_call(
        kernel,
        out_shape=tuple(outs),
        in_specs=[pl.BlockSpec(memory_space=pltpu.VMEM)] * len(args),
        out_specs=(pl.BlockSpec(memory_space=pltpu.VMEM),) * len(outs),
        scratch_shapes=list(scratch),
        cost_estimate=cost and pl.CostEstimate(flops=0, transcendentals=0, bytes_accessed=cost),
        compiler_params=pltpu.CompilerParams(vmem_limit_bytes=limit * 1024 * 1024),
    )(*args)


def images(orbitals, potential, chunks):
    nb, wx, wy, _ = orbitals.shape
    rows, wide, narrow = wx * wy, 12 * wy, 6 * wy
    p = orbitals.reshape(nb, rows, BLK)
    v = potential.reshape(rows, BLK)

    def shape(count, size):
        return jax.ShapeDtypeStruct((count, size, BLK), BF)

    whole = (
        slab(0, 0, wx, wy) + slab(0, -12, 0, wy) + slab(0, wx, wx + 12, wy)
        + slab(1, 0, wx, wy) + slab(1, -6, 0, wy) + slab(1, wx, wx + 6, wy)
    )
    middle = (
        slab(0, 0, wx, wy) + slab(0, -6, 0, wy) + slab(0, wx, wx + 6, wy) + slab(1, 0, wx, wy)
    )
    big = parts(plane_matrix(middle, whole, wy))
    small = parts(plane_matrix(slab(0, 0, wx, wy), middle, wy))
    line = parts(line_matrix(BLK))
    table = np.zeros((2 * len(middle) + 2 * max(rows, BLK), 5 * BLK), ml_dtypes.bfloat16)
    for k in range(2):
        table[k * len(middle) : (k + 1) * len(middle), : len(whole)] = big[k]
        at = 2 * len(middle) + k * rows
        table[at : at + rows, : len(middle)] = small[k]
        at = 2 * len(middle) + k * BLK
        table[at : at + BLK, -BLK:] = line[k]
    rounded = v.astype(BF)
    pair = [(0, 1), (1, 0)]
    other, other_v = lax.ppermute(p, "dy", pair), lax.ppermute(rounded, "dy", pair)
    (held,) = call(
        hold_kernel,
        [jax.ShapeDtypeStruct(table.shape, BF)],
        (jnp.asarray(table),),
        cost=4 * table.size,
    )
    last, first = call(
        functools.partial(edge_kernel, wide),
        [shape(nb + 1, wide + narrow)] * 2,
        (p, rounded, other, other_v),
    )
    count = lax.axis_size("dx")
    up = [(k, (k + 1) % count) for k in range(count)]
    low = lax.ppermute(last, "dx", up)
    high = lax.ppermute(first, "dx", [(b, a) for a, b in up])
    return call(
        functools.partial(stencil_kernel, wide),
        [shape(3 * nb * rows // chunks, chunks)],
        (p, v, other, other_v, low, high, held),
        [pltpu.VMEM((len(whole), 2 * BLK), BF)],
    )[0]


def swap(x, axes):
    return lax.all_to_all(x, axes, split_axis=0, concat_axis=0, tiled=True)


def spread(x, axes, size):
    return swap(jnp.broadcast_to(x[None], (size,) + x.shape), axes)


def pairs(nblk):
    return [(r, c) for r in range(nblk) for c in range(r, nblk)]


def tri(n):
    return lax.broadcasted_iota(jnp.int32, (n, n), 0), lax.broadcasted_iota(jnp.int32, (n, n), 1)


def panels(x_ref):
    return [
        jnp.concatenate([x_ref[k, h] for h in range(x_ref.shape[1])], axis=1) for k in range(3)
    ]


def gram_kernel(x_ref, rows_ref):
    p, i, r = panels(x_ref)
    n = p.shape[0]
    nblk = n // BLK
    qf = p.astype(F32) - TAU * i.astype(F32)
    q = qf.astype(BF)
    t = (qf - TAU * r.astype(F32)).astype(BF)

    def gram(a, b):
        return lax.dot_general(a, b, (((1,), (1,)), ((), ())), preferred_element_type=F32)

    s, g1, hw, hw2, w4 = gram(p, p), gram(i, p), gram(q, i), gram(r, q), gram(t, t)
    row, col = tri(n)
    at = 0
    for a, b in ((s, g1), (hw, hw2)):
        square = jnp.where(row > col, b, a).astype(BF)
        for c in range(nblk):
            rows_ref[at : at + n] = square[:, c * BLK : (c + 1) * BLK]
            at += n
    row, col = tri(BLK)

    def diagonal(g, k):
        block = g[k * BLK : (k + 1) * BLK, k * BLK : (k + 1) * BLK]
        return jnp.sum(jnp.where(row == col, block, 0.0), axis=0, keepdims=True)

    for k, c in pairs(nblk):
        block = w4[k * BLK : (k + 1) * BLK, c * BLK : (c + 1) * BLK]
        if k == c:
            first, second = diagonal(g1, k), diagonal(hw2, k)
            for at_row, line in (
                (BLK - 4, first), (BLK - 3, pltpu.roll(first, 64, 1)),
                (BLK - 2, second), (BLK - 1, pltpu.roll(second, 64, 1)),
            ):
                block = jnp.where((row == at_row) & (col < 64), line, block)
        rows_ref[at : at + BLK] = block.astype(BF)
        at += BLK


def reduced(rows):
    n_near = axes_size(NEAR)
    half = swap(rows.reshape(2, -1, BLK), "core").astype(F32).sum(0)
    part = swap(half.astype(BF).reshape(n_near, -1, BLK), NEAR).astype(F32).sum(0)
    part = spread(part, "zhi", lax.axis_size("zhi")).sum(0)
    part = spread(part, "yh", lax.axis_size("yh")).sum(0)
    half = spread(part, NEAR, n_near).reshape(-1, BLK)
    return spread(half, "core", 2).reshape(-1, BLK)


def axes_size(axes):
    size = 1
    for axis in axes:
        size *= lax.axis_size(axis)
    return size


def dot(a, b):
    return jnp.dot(a, b, preferred_element_type=F32)


def split(x):
    high = x.astype(BF)
    return high, (x - high.astype(F32)).astype(BF)


def algebra_kernel(volume, rows_ref, x_ref, psi_ref, h_ref, mats):
    n = x_ref.shape[2]
    nblk = n // BLK
    row, col = tri(BLK)

    def put(g, r, c, tile):
        mats[g, r * BLK : (r + 1) * BLK, c * BLK : (c + 1) * BLK] = tile

    at = 2 * nblk * n
    lines = {}
    for r, c in pairs(nblk):
        tile = rows_ref[at : at + BLK] * volume
        at += BLK
        if r == c:
            for g, k in ((1, BLK - 4), (3, BLK - 2)):
                second = pltpu.roll(tile[k + 1 : k + 2], 64, 1)
                lines[g, r] = jnp.where(col[:1] < 64, tile[k : k + 1], second)
            put(4, r, r, jnp.where(row <= col, tile, tile.T))
        else:
            put(4, r, c, tile)
            put(4, c, r, tile.T)
    for g in (0, 2):
        for r in range(nblk):
            for c in range(nblk):
                at = (g // 2 * nblk + c) * n + r * BLK
                tile = rows_ref[at : at + BLK] * volume
                flip = tile.T
                if r == c:
                    put(g, r, r, jnp.where(row <= col, tile, flip))
                    other = jnp.where(row >= col, tile, flip)
                    put(g + 1, r, r, jnp.where(row == col, lines[g + 1, r], other))
                else:
                    to = g if r < c else g + 1
                    put(to, r, c, tile)
                    put(to, c, r, flip)
    s, g1, hw, hw2, w4 = (mats[g] for g in range(NGRAM))
    w1 = s - TAU * g1
    w2 = w1 - TAU * hw
    w3 = w2 - TAU * hw2
    row, col = tri(n)
    diag = jnp.where(row == col, 1.5, 0.0).astype(F32)

    def full(a, x):
        high, low = split(x)
        return dot(a[0], high) + dot(a[0], low) + dot(a[1], high)

    def outer(high, middle, low, h):
        b = middle + (0.5 * TAU) * dot(h, low.astype(BF))
        b = TAU * dot(b.astype(BF), h)
        return high + b + b.T

    h = g1.astype(BF)
    c1 = outer(w2, w1, s, h)
    m1 = split(diag - 0.5 * c1)

    def both(x):
        return full(m1, full(m1, x).T)

    def both_rounded(x):
        x = x.astype(BF)
        x = (dot(m1[0], x) + dot(m1[1], x)).T.astype(BF)
        return dot(m1[0], x) + dot(m1[1], x)

    h2 = both(outer(hw2, hw, g1, h))
    h_ref[...] = h2
    s1 = both_rounded(c1)
    w2b = both_rounded(outer(w4, w3, w2, h))
    hh = h2.astype(BF)
    m2 = split(diag - 0.5 * outer(w2b, s1 - TAU * h2, s1, hh))

    p, i, r = panels(x_ref)
    hp = TAU * dot(h, p)
    hq = hp - (TAU * TAU) * dot(h, i)
    q = p.astype(F32) - TAU * i.astype(F32)
    t = q - TAU * r.astype(F32)
    psi1 = full(m1, q + hp)
    wpsi1 = full(m1, t + hq)
    psi2 = full(m2, wpsi1 + TAU * dot(hh, psi1.astype(BF))).astype(BF)
    group = psi_ref.shape[1]
    nh = x_ref.shape[1]
    for b in range(n // group):
        for h in range(nh):
            psi_ref[b * nh + h] = psi2[b * group : (b + 1) * group, h * BLK : (h + 1) * BLK]


def algebra(rows, x, volume, n_band):
    n = x.shape[2]
    count = n // n_band * x.shape[1]
    return call(
        functools.partial(algebra_kernel, volume),
        [jax.ShapeDtypeStruct((count, n_band, BLK), BF), jax.ShapeDtypeStruct((n, n), F32)],
        (rows, x),
        [pltpu.VMEM((NGRAM, n, n), F32)],
        48,
    )


def per_device(orbitals, potential):
    shape = orbitals.shape
    nb = shape[0]
    n_band = axes_size(BAND)
    cells = shape[1] * shape[2] * shape[3]
    bands = nb * n_band
    chunk = cells // n_band
    volume = 1.0 / (cells * lax.axis_size("dx") * lax.axis_size("dy"))

    send = images(orbitals, potential, n_band).transpose(1, 0, 2)
    got = swap(send, BAND).transpose(1, 0, 2)
    x = got.reshape(3, chunk // BLK, bands, BLK)

    count = bands // BLK * 2 * bands + len(pairs(bands // BLK)) * BLK
    (rows,) = call(gram_kernel, [jax.ShapeDtypeStruct((count, BLK), BF)], (x,))
    psi2, h2 = algebra(reduced(rows), x, volume, n_band)

    back = swap(psi2.transpose(1, 0, 2), BAND).transpose(1, 0, 2)
    mine = lax.dynamic_index_in_dim(h2.reshape(nb, n_band, bands), lax.axis_index(BAND), 1, False)
    columns = mine.reshape(nb, nb, n_band).transpose(2, 1, 0).reshape(bands, nb)
    return back.reshape(shape), columns


def solution(mesh):
    n_band, n_dx, n_dy = mesh.devices.shape
    near = min(2, n_band // 2)
    far = min(4, n_band // 2 // near)
    fine = Mesh(mesh.devices.reshape(-1, far, near, 2, n_dx, n_dy), BAND + ("dx", "dy"))
    in_specs = (P(BAND, "dx", "dy", None), P("dx", "dy", None))
    out_specs = (P(BAND, "dx", "dy", None), P(None, BAND))
    return jax.shard_map(
        per_device, mesh=fine, in_specs=in_specs, out_specs=out_specs, check_vma=False
    )
```

```python
import functools

import jax
import jax.numpy as jnp
import ml_dtypes
import numpy as np
from jax import lax
from jax.experimental import pallas as pl
from jax.experimental.pallas import tpu as pltpu
from jax.sharding import Mesh, PartitionSpec as P

COEFFS = (
    -5369.0 / 1800.0,
    12.0 / 7.0,
    -15.0 / 56.0,
    10.0 / 189.0,
    -1.0 / 112.0,
    2.0 / 1925.0,
    -1.0 / 16632.0,
)
TAU = 0.1
BF = jnp.bfloat16
F32 = jnp.float32
BAND = ("zhi", "yh", "yl", "core")
NEAR = ("dx", "dy", "yl")
BLK = 128
NGRAM = 5


def parts(matrix):
    high = matrix.astype(np.float32).astype(ml_dtypes.bfloat16)
    return high, (matrix - high.astype(np.float64)).astype(np.float32).astype(ml_dtypes.bfloat16)


def plane_matrix(out_rows, in_rows, wy):
    where = {row: k for k, row in enumerate(in_rows)}
    matrix = np.zeros((len(out_rows), len(in_rows)))
    for k, (side, x, y) in enumerate(out_rows):
        matrix[k, where[side, x, y]] += -1.5 * COEFFS[0]
        for offset in range(1, 7):
            for shift in (offset, -offset):
                matrix[k, where[side, x + shift, y]] += -0.5 * COEFFS[offset]
                at = (side * wy + y + shift) % (2 * wy)
                matrix[k, where[at // wy, x, at % wy]] += -0.5 * COEFFS[offset]
    return matrix


def line_matrix(length):
    matrix = np.zeros((length, length))
    at = np.arange(length)
    for offset in range(1, 7):
        for shift in (offset, -offset):
            matrix[at, (at + shift) % length] += -0.5 * COEFFS[offset]
    return matrix


def slab(side, first, last, wy):
    return [(side, x, y) for x in range(first, last) for y in range(wy)]


def hold_kernel(table_ref, held_ref):
    held_ref[...] = table_ref[...]


def edge_kernel(wide, p_ref, v_ref, other_ref, other_v_ref, last_ref, first_ref):
    nb, rows, _ = p_ref.shape
    narrow = last_ref.shape[1] - wide
    last_ref[:nb, :wide] = p_ref[:, rows - wide :]
    first_ref[:nb, :wide] = p_ref[:, :wide]
    last_ref[:nb, wide:] = other_ref[:, rows - narrow :]
    first_ref[:nb, wide:] = other_ref[:, :narrow]
    last_ref[nb, :wide] = v_ref[rows - wide :]
    first_ref[nb, :wide] = v_ref[:wide]
    last_ref[nb, wide:] = other_v_ref[rows - narrow :]
    first_ref[nb, wide:] = other_v_ref[:narrow]


def stencil_kernel(
    wide, p_ref, v_ref, other_ref, other_v_ref, lo_ref, hi_ref, table_ref, out_ref, field
):
    size = field.shape[0]
    nb, rows, _ = p_ref.shape
    narrow = lo_ref.shape[1] - wide
    middle = 2 * rows + 2 * narrow
    last = 2 * middle + rows
    end = last + rows
    corner = table_ref.shape[1] - BLK
    a1h, a1l = table_ref[:middle, :size], table_ref[middle : 2 * middle, :size]
    a2h, a2l = table_ref[2 * middle : last, :middle], table_ref[last:end, :middle]
    zh = table_ref[2 * middle : 2 * middle + BLK, corner:]
    zl = table_ref[2 * middle + BLK : 2 * middle + 2 * BLK, corner:]

    def along_z(x):
        halves = (x[:, :BLK], x[:, BLK:])
        return jnp.concatenate([dot(h, zh) + dot(h, zl) for h in halves], axis=1)

    def around(low, high, other):
        return jnp.concatenate([low[wide - narrow : wide], high[:narrow], other], axis=0).astype(F32)

    v = jnp.concatenate([v_ref[...], around(lo_ref[nb], hi_ref[nb], other_v_ref[...])], axis=0)
    v = jnp.concatenate([v, v], axis=1)
    chunks = out_ref.shape[1]
    parts_out = rows // chunks
    for b in range(0, nb, 2):
        at = 0
        for ref, first, size in (
            (p_ref, 0, rows), (lo_ref, 0, wide), (hi_ref, 0, wide),
            (other_ref, 0, rows), (lo_ref, wide, narrow), (hi_ref, wide, narrow),
        ):
            field[at : at + size, :BLK] = ref[b, first : first + size]
            field[at : at + size, BLK:] = ref[b + 1, first : first + size]
            at += size
        f = field[...]
        centre = jnp.concatenate(
            [
                f[:rows],
                f[rows + wide - narrow : rows + wide],
                f[rows + wide : rows + wide + narrow],
                f[rows + 2 * wide : 2 * rows + 2 * wide],
            ],
            axis=0,
        )
        image = dot(a1h, f) + dot(a1l, f) + along_z(centre)
        centre = centre.astype(F32)
        image = (image + v * centre).astype(BF)
        q = (centre - TAU * image.astype(F32)).astype(BF)
        own = q[:rows]
        second = dot(a2h, q) + dot(a2l, q) + along_z(own)
        second = (second + v[:rows] * own.astype(F32)).astype(BF)
        for k, x in enumerate((f[:rows], image[:rows], second)):
            for h in range(parts_out):
                for j in range(2):
                    block = x[h * chunks : (h + 1) * chunks, j * BLK : (j + 1) * BLK]
                    out_ref[(k * parts_out + h) * nb + b + j] = block


def call(kernel, outs, args, scratch=(), limit=32, cost=None):
    return pl.pallas_call(
        kernel,
        out_shape=tuple(outs),
        in_specs=[pl.BlockSpec(memory_space=pltpu.VMEM)] * len(args),
        out_specs=(pl.BlockSpec(memory_space=pltpu.VMEM),) * len(outs),
        scratch_shapes=list(scratch),
        cost_estimate=cost and pl.CostEstimate(flops=0, transcendentals=0, bytes_accessed=cost),
        compiler_params=pltpu.CompilerParams(vmem_limit_bytes=limit * 1024 * 1024),
    )(*args)


def images(orbitals, potential, chunks):
    nb, wx, wy, _ = orbitals.shape
    rows, wide, narrow = wx * wy, 12 * wy, 6 * wy
    p = orbitals.reshape(nb, rows, BLK)
    v = potential.reshape(rows, BLK)

    def shape(count, size):
        return jax.ShapeDtypeStruct((count, size, BLK), BF)

    whole = (
        slab(0, 0, wx, wy) + slab(0, -12, 0, wy) + slab(0, wx, wx + 12, wy)
        + slab(1, 0, wx, wy) + slab(1, -6, 0, wy) + slab(1, wx, wx + 6, wy)
    )
    middle = (
        slab(0, 0, wx, wy) + slab(0, -6, 0, wy) + slab(0, wx, wx + 6, wy) + slab(1, 0, wx, wy)
    )
    big = parts(plane_matrix(middle, whole, wy))
    small = parts(plane_matrix(slab(0, 0, wx, wy), middle, wy))
    line = parts(line_matrix(BLK))
    table = np.zeros((2 * len(middle) + 2 * max(rows, BLK), 5 * BLK), ml_dtypes.bfloat16)
    for k in range(2):
        table[k * len(middle) : (k + 1) * len(middle), : len(whole)] = big[k]
        at = 2 * len(middle) + k * rows
        table[at : at + rows, : len(middle)] = small[k]
        at = 2 * len(middle) + k * BLK
        table[at : at + BLK, -BLK:] = line[k]
    rounded = v.astype(BF)
    pair = [(0, 1), (1, 0)]
    other, other_v = lax.ppermute(p, "dy", pair), lax.ppermute(rounded, "dy", pair)
    (held,) = call(
        hold_kernel,
        [jax.ShapeDtypeStruct(table.shape, BF)],
        (jnp.asarray(table),),
        cost=4 * table.size,
    )
    last, first = call(
        functools.partial(edge_kernel, wide),
        [shape(nb + 1, wide + narrow)] * 2,
        (p, rounded, other, other_v),
    )
    count = lax.axis_size("dx")
    up = [(k, (k + 1) % count) for k in range(count)]
    low = lax.ppermute(last, "dx", up)
    high = lax.ppermute(first, "dx", [(b, a) for a, b in up])
    return call(
        functools.partial(stencil_kernel, wide),
        [shape(3 * nb * rows // chunks, chunks)],
        (p, v, other, other_v, low, high, held),
        [pltpu.VMEM((len(whole), 2 * BLK), BF)],
    )[0]


def swap(x, axes):
    return lax.all_to_all(x, axes, split_axis=0, concat_axis=0, tiled=True)


def spread(x, axes, size):
    return swap(jnp.broadcast_to(x[None], (size,) + x.shape), axes)


def pairs(nblk):
    return [(r, c) for r in range(nblk) for c in range(r, nblk)]


def tri(n):
    return lax.broadcasted_iota(jnp.int32, (n, n), 0), lax.broadcasted_iota(jnp.int32, (n, n), 1)


def panels(x_ref):
    return [
        jnp.concatenate([x_ref[k, h] for h in range(x_ref.shape[1])], axis=1) for k in range(3)
    ]


def core_halves(count):
    half = count // 2
    core = lax.axis_index("core")
    return [pl.ds(pl.multiple_of(c * half, BLK), half) for c in (core, 1 - core)]


def gram_kernel(x_ref, mine_ref, theirs_ref, rows_ref):
    p, i, r = panels(x_ref)
    n = p.shape[0]
    nblk = n // BLK
    qf = p.astype(F32) - TAU * i.astype(F32)
    q = qf.astype(BF)
    t = (qf - TAU * r.astype(F32)).astype(BF)

    def gram(a, b):
        return lax.dot_general(a, b, (((1,), (1,)), ((), ())), preferred_element_type=F32)

    s, g1, hw, hw2, w4 = gram(p, p), gram(i, p), gram(q, i), gram(r, q), gram(t, t)
    row, col = tri(n)
    at = 0
    for a, b in ((s, g1), (hw, hw2)):
        square = jnp.where(row > col, b, a).astype(BF)
        for c in range(nblk):
            rows_ref[at : at + n] = square[:, c * BLK : (c + 1) * BLK]
            at += n
    row, col = tri(BLK)

    def diagonal(g, k):
        block = g[k * BLK : (k + 1) * BLK, k * BLK : (k + 1) * BLK]
        return jnp.sum(jnp.where(row == col, block, 0.0), axis=0, keepdims=True)

    for k, c in pairs(nblk):
        block = w4[k * BLK : (k + 1) * BLK, c * BLK : (c + 1) * BLK]
        if k == c:
            first, second = diagonal(g1, k), diagonal(hw2, k)
            for at_row, line in (
                (BLK - 4, first), (BLK - 3, pltpu.roll(first, 64, 1)),
                (BLK - 2, second), (BLK - 1, pltpu.roll(second, 64, 1)),
            ):
                block = jnp.where((row == at_row) & (col < 64), line, block)
        rows_ref[at : at + BLK] = block.astype(BF)
        at += BLK
    mine, theirs = core_halves(rows_ref.shape[0])
    mine_ref[...] = rows_ref[mine]
    theirs_ref[...] = rows_ref[theirs]


def reduced(mine, theirs):
    n_near = axes_size(NEAR)
    pair = [(0, 1), (1, 0)]
    half = mine.astype(F32) + lax.ppermute(theirs, "core", pair).astype(F32)
    part = swap(half.astype(BF).reshape(n_near, -1, BLK), NEAR).astype(F32).sum(0)
    part = spread(part, "zhi", lax.axis_size("zhi")).sum(0)
    part = spread(part, "yh", lax.axis_size("yh")).sum(0)
    half = spread(part, NEAR, n_near).reshape(-1, BLK)
    return half, lax.ppermute(half, "core", pair)


def axes_size(axes):
    size = 1
    for axis in axes:
        size *= lax.axis_size(axis)
    return size


def dot(a, b):
    return jnp.dot(a, b, preferred_element_type=F32)


def split(x):
    high = x.astype(BF)
    return high, (x - high.astype(F32)).astype(BF)


def algebra_kernel(volume, mine_ref, theirs_ref, x_ref, psi_ref, h_ref, mats, rows_ref):
    n = x_ref.shape[2]
    nblk = n // BLK
    mine, theirs = core_halves(rows_ref.shape[0])
    rows_ref[mine] = mine_ref[...]
    rows_ref[theirs] = theirs_ref[...]
    row, col = tri(BLK)

    def put(g, r, c, tile):
        mats[g, r * BLK : (r + 1) * BLK, c * BLK : (c + 1) * BLK] = tile

    at = 2 * nblk * n
    lines = {}
    for r, c in pairs(nblk):
        tile = rows_ref[at : at + BLK] * volume
        at += BLK
        if r == c:
            for g, k in ((1, BLK - 4), (3, BLK - 2)):
                second = pltpu.roll(tile[k + 1 : k + 2], 64, 1)
                lines[g, r] = jnp.where(col[:1] < 64, tile[k : k + 1], second)
            put(4, r, r, jnp.where(row <= col, tile, tile.T))
        else:
            put(4, r, c, tile)
            put(4, c, r, tile.T)
    for g in (0, 2):
        for r in range(nblk):
            for c in range(nblk):
                at = (g // 2 * nblk + c) * n + r * BLK
                tile = rows_ref[at : at + BLK] * volume
                flip = tile.T
                if r == c:
                    put(g, r, r, jnp.where(row <= col, tile, flip))
                    other = jnp.where(row >= col, tile, flip)
                    put(g + 1, r, r, jnp.where(row == col, lines[g + 1, r], other))
                else:
                    to = g if r < c else g + 1
                    put(to, r, c, tile)
                    put(to, c, r, flip)
    s, g1, hw, hw2, w4 = (mats[g] for g in range(NGRAM))
    w1 = s - TAU * g1
    w2 = w1 - TAU * hw
    w3 = w2 - TAU * hw2
    row, col = tri(n)
    diag = jnp.where(row == col, 1.5, 0.0).astype(F32)

    def full(a, x):
        high, low = split(x)
        return dot(a[0], high) + dot(a[0], low) + dot(a[1], high)

    def outer(high, middle, low, h):
        b = middle + (0.5 * TAU) * dot(h, low.astype(BF))
        b = TAU * dot(b.astype(BF), h)
        return high + b + b.T

    h = g1.astype(BF)
    c1 = outer(w2, w1, s, h)
    m1 = split(diag - 0.5 * c1)

    def both(x):
        return full(m1, full(m1, x).T)

    def both_rounded(x):
        x = x.astype(BF)
        x = (dot(m1[0], x) + dot(m1[1], x)).T.astype(BF)
        return dot(m1[0], x) + dot(m1[1], x)

    h2 = both(outer(hw2, hw, g1, h))
    h_ref[...] = h2
    s1 = both_rounded(c1)
    w2b = both_rounded(outer(w4, w3, w2, h))
    hh = h2.astype(BF)
    m2 = split(diag - 0.5 * outer(w2b, s1 - TAU * h2, s1, hh))

    p, i, r = panels(x_ref)
    hp = TAU * dot(h, p)
    hq = hp - (TAU * TAU) * dot(h, i)
    q = p.astype(F32) - TAU * i.astype(F32)
    t = q - TAU * r.astype(F32)
    psi1 = full(m1, q + hp)
    wpsi1 = full(m1, t + hq)
    psi2 = full(m2, wpsi1 + TAU * dot(hh, psi1.astype(BF))).astype(BF)
    group = psi_ref.shape[1]
    nh = x_ref.shape[1]
    for b in range(n // group):
        for h in range(nh):
            psi_ref[b * nh + h] = psi2[b * group : (b + 1) * group, h * BLK : (h + 1) * BLK]


def algebra(mine, theirs, x, volume, n_band):
    n = x.shape[2]
    count = n // n_band * x.shape[1]
    return call(
        functools.partial(algebra_kernel, volume),
        [jax.ShapeDtypeStruct((count, n_band, BLK), BF), jax.ShapeDtypeStruct((n, n), F32)],
        (mine, theirs, x),
        [pltpu.VMEM((NGRAM, n, n), F32), pltpu.VMEM((2 * mine.shape[0], BLK), F32)],
        48,
    )


def per_device(orbitals, potential):
    shape = orbitals.shape
    nb = shape[0]
    n_band = axes_size(BAND)
    cells = shape[1] * shape[2] * shape[3]
    bands = nb * n_band
    chunk = cells // n_band
    volume = 1.0 / (cells * lax.axis_size("dx") * lax.axis_size("dy"))

    send = images(orbitals, potential, n_band).transpose(1, 0, 2)
    got = swap(send, BAND).transpose(1, 0, 2)
    x = got.reshape(3, chunk // BLK, bands, BLK)

    count = bands // BLK * 2 * bands + len(pairs(bands // BLK)) * BLK
    halves = call(
        gram_kernel,
        [jax.ShapeDtypeStruct((count // 2, BLK), BF)] * 2,
        (x,),
        [pltpu.VMEM((count, BLK), BF)],
    )
    psi2, h2 = algebra(*reduced(*halves), x, volume, n_band)

    back = swap(psi2.transpose(1, 0, 2), BAND).transpose(1, 0, 2)
    mine = lax.dynamic_index_in_dim(h2.reshape(nb, n_band, bands), lax.axis_index(BAND), 1, False)
    columns = mine.reshape(nb, nb, n_band).transpose(2, 1, 0).reshape(bands, nb)
    return back.reshape(shape), columns


def solution(mesh):
    n_band, n_dx, n_dy = mesh.devices.shape
    near = min(2, n_band // 2)
    far = min(4, n_band // 2 // near)
    fine = Mesh(mesh.devices.reshape(-1, far, near, 2, n_dx, n_dy), BAND + ("dx", "dy"))
    in_specs = (P(BAND, "dx", "dy", None), P("dx", "dy", None))
    out_specs = (P(BAND, "dx", "dy", None), P(None, BAND))
    return jax.shard_map(
        per_device, mesh=fine, in_specs=in_specs, out_specs=out_specs, check_vma=False
    )
```

```python
import functools

import jax
import jax.numpy as jnp
import ml_dtypes
import numpy as np
from jax import lax
from jax.experimental import pallas as pl
from jax.experimental.pallas import tpu as pltpu
from jax.sharding import Mesh, PartitionSpec as P

COEFFS = (
    -5369.0 / 1800.0,
    12.0 / 7.0,
    -15.0 / 56.0,
    10.0 / 189.0,
    -1.0 / 112.0,
    2.0 / 1925.0,
    -1.0 / 16632.0,
)
TAU = 0.1
BF = jnp.bfloat16
F32 = jnp.float32
BAND = ("zhi", "yh", "yl", "core")
NEAR = ("dx", "dy", "yl")
BLK = 128
NGRAM = 5


def parts(matrix):
    high = matrix.astype(np.float32).astype(ml_dtypes.bfloat16)
    return high, (matrix - high.astype(np.float64)).astype(np.float32).astype(ml_dtypes.bfloat16)


def plane_matrix(out_rows, in_rows, wy):
    where = {row: k for k, row in enumerate(in_rows)}
    matrix = np.zeros((len(out_rows), len(in_rows)))
    for k, (side, x, y) in enumerate(out_rows):
        matrix[k, where[side, x, y]] += -1.5 * COEFFS[0]
        for offset in range(1, 7):
            for shift in (offset, -offset):
                matrix[k, where[side, x + shift, y]] += -0.5 * COEFFS[offset]
                at = (side * wy + y + shift) % (2 * wy)
                matrix[k, where[at // wy, x, at % wy]] += -0.5 * COEFFS[offset]
    return matrix


def line_matrix(length):
    matrix = np.zeros((length, length))
    at = np.arange(length)
    for offset in range(1, 7):
        for shift in (offset, -offset):
            matrix[at, (at + shift) % length] += -0.5 * COEFFS[offset]
    return matrix


def slab(side, first, last, wy):
    return [(side, x, y) for x in range(first, last) for y in range(wy)]


def hold_kernel(table_ref, held_ref):
    held_ref[...] = table_ref[...]


def edge_kernel(wide, p_ref, v_ref, other_ref, other_v_ref, last_ref, first_ref):
    nb, rows, _ = p_ref.shape
    narrow = last_ref.shape[1] - wide
    last_ref[:nb, :wide] = p_ref[:, rows - wide :]
    first_ref[:nb, :wide] = p_ref[:, :wide]
    last_ref[:nb, wide:] = other_ref[:, rows - narrow :]
    first_ref[:nb, wide:] = other_ref[:, :narrow]
    last_ref[nb, :wide] = v_ref[rows - wide :]
    first_ref[nb, :wide] = v_ref[:wide]
    last_ref[nb, wide:] = other_v_ref[rows - narrow :]
    first_ref[nb, wide:] = other_v_ref[:narrow]


def stencil_kernel(
    wide, p_ref, v_ref, other_ref, other_v_ref, lo_ref, hi_ref, table_ref, out_ref, field
):
    size = field.shape[0]
    nb, rows, _ = p_ref.shape
    narrow = lo_ref.shape[1] - wide
    middle = 2 * rows + 2 * narrow
    last = 2 * middle + rows
    end = last + rows
    corner = table_ref.shape[1] - BLK
    a1h, a1l = table_ref[:middle, :size], table_ref[middle : 2 * middle, :size]
    a2h, a2l = table_ref[2 * middle : last, :middle], table_ref[last:end, :middle]
    zh = table_ref[2 * middle : 2 * middle + BLK, corner:]
    zl = table_ref[2 * middle + BLK : 2 * middle + 2 * BLK, corner:]

    def along_z(x):
        halves = (x[:, :BLK], x[:, BLK:])
        return jnp.concatenate([dot(h, zh) + dot(h, zl) for h in halves], axis=1)

    def around(low, high, other):
        return jnp.concatenate([low[wide - narrow : wide], high[:narrow], other], axis=0).astype(F32)

    v = jnp.concatenate([v_ref[...], around(lo_ref[nb], hi_ref[nb], other_v_ref[...])], axis=0)
    v = jnp.concatenate([v, v], axis=1)
    chunks = out_ref.shape[1]
    parts_out = rows // chunks
    for b in range(0, nb, 2):
        at = 0
        for ref, first, size in (
            (p_ref, 0, rows), (lo_ref, 0, wide), (hi_ref, 0, wide),
            (other_ref, 0, rows), (lo_ref, wide, narrow), (hi_ref, wide, narrow),
        ):
            field[at : at + size, :BLK] = ref[b, first : first + size]
            field[at : at + size, BLK:] = ref[b + 1, first : first + size]
            at += size
        f = field[...]
        centre = jnp.concatenate(
            [
                f[:rows],
                f[rows + wide - narrow : rows + wide],
                f[rows + wide : rows + wide + narrow],
                f[rows + 2 * wide : 2 * rows + 2 * wide],
            ],
            axis=0,
        )
        image = dot(a1h, f) + dot(a1l, f) + along_z(centre)
        centre = centre.astype(F32)
        image = (image + v * centre).astype(BF)
        q = (centre - TAU * image.astype(F32)).astype(BF)
        own = q[:rows]
        second = dot(a2h, q) + dot(a2l, q) + along_z(own)
        second = (second + v[:rows] * own.astype(F32)).astype(BF)
        for k, x in enumerate((f[:rows], image[:rows], second)):
            for h in range(parts_out):
                for j in range(2):
                    block = x[h * chunks : (h + 1) * chunks, j * BLK : (j + 1) * BLK]
                    out_ref[(k * parts_out + h) * nb + b + j] = block


def call(kernel, outs, args, scratch=(), limit=32, cost=None):
    return pl.pallas_call(
        kernel,
        out_shape=tuple(outs),
        in_specs=[pl.BlockSpec(memory_space=pltpu.VMEM)] * len(args),
        out_specs=(pl.BlockSpec(memory_space=pltpu.VMEM),) * len(outs),
        scratch_shapes=list(scratch),
        cost_estimate=cost and pl.CostEstimate(flops=0, transcendentals=0, bytes_accessed=cost),
        compiler_params=pltpu.CompilerParams(vmem_limit_bytes=limit * 1024 * 1024),
    )(*args)


def images(orbitals, potential, chunks):
    nb, wx, wy, _ = orbitals.shape
    rows, wide, narrow = wx * wy, 12 * wy, 6 * wy
    p = orbitals.reshape(nb, rows, BLK)
    v = potential.reshape(rows, BLK)

    def shape(count, size):
        return jax.ShapeDtypeStruct((count, size, BLK), BF)

    whole = (
        slab(0, 0, wx, wy) + slab(0, -12, 0, wy) + slab(0, wx, wx + 12, wy)
        + slab(1, 0, wx, wy) + slab(1, -6, 0, wy) + slab(1, wx, wx + 6, wy)
    )
    middle = (
        slab(0, 0, wx, wy) + slab(0, -6, 0, wy) + slab(0, wx, wx + 6, wy) + slab(1, 0, wx, wy)
    )
    big = parts(plane_matrix(middle, whole, wy))
    small = parts(plane_matrix(slab(0, 0, wx, wy), middle, wy))
    line = parts(line_matrix(BLK))
    table = np.zeros((2 * len(middle) + 2 * max(rows, BLK), 5 * BLK), ml_dtypes.bfloat16)
    for k in range(2):
        table[k * len(middle) : (k + 1) * len(middle), : len(whole)] = big[k]
        at = 2 * len(middle) + k * rows
        table[at : at + rows, : len(middle)] = small[k]
        at = 2 * len(middle) + k * BLK
        table[at : at + BLK, -BLK:] = line[k]
    rounded = v.astype(BF)
    pair = [(0, 1), (1, 0)]
    other, other_v = lax.ppermute(p, "dy", pair), lax.ppermute(rounded, "dy", pair)
    (psi,) = call(hold_kernel, [shape(nb, rows)], (p,), cost=4 * p.size)
    (held,) = call(
        hold_kernel,
        [jax.ShapeDtypeStruct(table.shape, BF)],
        (jnp.asarray(table),),
        cost=4 * table.size,
    )
    last, first = call(
        functools.partial(edge_kernel, wide),
        [shape(nb + 1, wide + narrow)] * 2,
        (psi, rounded, other, other_v),
    )
    count = lax.axis_size("dx")
    up = [(k, (k + 1) % count) for k in range(count)]
    low = lax.ppermute(last, "dx", up)
    high = lax.ppermute(first, "dx", [(b, a) for a, b in up])
    return call(
        functools.partial(stencil_kernel, wide),
        [shape(3 * nb * rows // chunks, chunks)],
        (psi, v, other, other_v, low, high, held),
        [pltpu.VMEM((len(whole), 2 * BLK), BF)],
    )[0]


def swap(x, axes):
    return lax.all_to_all(x, axes, split_axis=0, concat_axis=0, tiled=True)


def spread(x, axes, size):
    return swap(jnp.broadcast_to(x[None], (size,) + x.shape), axes)


def pairs(nblk):
    return [(r, c) for r in range(nblk) for c in range(r, nblk)]


def tri(n):
    return lax.broadcasted_iota(jnp.int32, (n, n), 0), lax.broadcasted_iota(jnp.int32, (n, n), 1)


def panels(x_ref):
    return [
        jnp.concatenate([x_ref[k, h] for h in range(x_ref.shape[1])], axis=1) for k in range(3)
    ]


def core_halves(count):
    half = count // 2
    core = lax.axis_index("core")
    return [pl.ds(pl.multiple_of(c * half, BLK), half) for c in (core, 1 - core)]


def gram_kernel(x_ref, mine_ref, theirs_ref, rows_ref):
    p, i, r = panels(x_ref)
    n = p.shape[0]
    nblk = n // BLK
    qf = p.astype(F32) - TAU * i.astype(F32)
    q = qf.astype(BF)
    t = (qf - TAU * r.astype(F32)).astype(BF)

    def gram(a, b):
        return lax.dot_general(a, b, (((1,), (1,)), ((), ())), preferred_element_type=F32)

    s, g1, hw, hw2, w4 = gram(p, p), gram(i, p), gram(q, i), gram(r, q), gram(t, t)
    row, col = tri(n)
    at = 0
    for a, b in ((s, g1), (hw, hw2)):
        square = jnp.where(row > col, b, a).astype(BF)
        for c in range(nblk):
            rows_ref[at : at + n] = square[:, c * BLK : (c + 1) * BLK]
            at += n
    row, col = tri(BLK)

    def diagonal(g, k):
        block = g[k * BLK : (k + 1) * BLK, k * BLK : (k + 1) * BLK]
        return jnp.sum(jnp.where(row == col, block, 0.0), axis=0, keepdims=True)

    for k, c in pairs(nblk):
        block = w4[k * BLK : (k + 1) * BLK, c * BLK : (c + 1) * BLK]
        if k == c:
            first, second = diagonal(g1, k), diagonal(hw2, k)
            for at_row, line in (
                (BLK - 4, first), (BLK - 3, pltpu.roll(first, 64, 1)),
                (BLK - 2, second), (BLK - 1, pltpu.roll(second, 64, 1)),
            ):
                block = jnp.where((row == at_row) & (col < 64), line, block)
        rows_ref[at : at + BLK] = block.astype(BF)
        at += BLK
    mine, theirs = core_halves(rows_ref.shape[0])
    mine_ref[...] = rows_ref[mine]
    theirs_ref[...] = rows_ref[theirs]


def reduced(mine, theirs):
    n_near = axes_size(NEAR)
    pair = [(0, 1), (1, 0)]
    half = mine.astype(F32) + lax.ppermute(theirs, "core", pair).astype(F32)
    part = swap(half.astype(BF).reshape(n_near, -1, BLK), NEAR).astype(F32).sum(0)
    part = spread(part, "zhi", lax.axis_size("zhi")).sum(0)
    part = spread(part, "yh", lax.axis_size("yh")).sum(0)
    half = spread(part, NEAR, n_near).reshape(-1, BLK)
    return half, lax.ppermute(half, "core", pair)


def axes_size(axes):
    size = 1
    for axis in axes:
        size *= lax.axis_size(axis)
    return size


def dot(a, b):
    return jnp.dot(a, b, preferred_element_type=F32)


def split(x):
    high = x.astype(BF)
    return high, (x - high.astype(F32)).astype(BF)


def algebra_kernel(volume, mine_ref, theirs_ref, x_ref, psi_ref, h_ref, mats, rows_ref):
    n = x_ref.shape[2]
    nblk = n // BLK
    mine, theirs = core_halves(rows_ref.shape[0])
    rows_ref[mine] = mine_ref[...]
    rows_ref[theirs] = theirs_ref[...]
    row, col = tri(BLK)

    def put(g, r, c, tile):
        mats[g, r * BLK : (r + 1) * BLK, c * BLK : (c + 1) * BLK] = tile

    at = 2 * nblk * n
    lines = {}
    for r, c in pairs(nblk):
        tile = rows_ref[at : at + BLK] * volume
        at += BLK
        if r == c:
            for g, k in ((1, BLK - 4), (3, BLK - 2)):
                second = pltpu.roll(tile[k + 1 : k + 2], 64, 1)
                lines[g, r] = jnp.where(col[:1] < 64, tile[k : k + 1], second)
            put(4, r, r, jnp.where(row <= col, tile, tile.T))
        else:
            put(4, r, c, tile)
            put(4, c, r, tile.T)
    for g in (0, 2):
        for r in range(nblk):
            for c in range(nblk):
                at = (g // 2 * nblk + c) * n + r * BLK
                tile = rows_ref[at : at + BLK] * volume
                flip = tile.T
                if r == c:
                    put(g, r, r, jnp.where(row <= col, tile, flip))
                    other = jnp.where(row >= col, tile, flip)
                    put(g + 1, r, r, jnp.where(row == col, lines[g + 1, r], other))
                else:
                    to = g if r < c else g + 1
                    put(to, r, c, tile)
                    put(to, c, r, flip)
    s, g1, hw, hw2, w4 = (mats[g] for g in range(NGRAM))
    w1 = s - TAU * g1
    w2 = w1 - TAU * hw
    w3 = w2 - TAU * hw2
    row, col = tri(n)
    diag = jnp.where(row == col, 1.5, 0.0).astype(F32)

    def full(a, x):
        high, low = split(x)
        return dot(a[0], high) + dot(a[0], low) + dot(a[1], high)

    def outer(high, middle, low, h):
        b = middle + (0.5 * TAU) * dot(h, low.astype(BF))
        b = TAU * dot(b.astype(BF), h)
        return high + b + b.T

    h = g1.astype(BF)
    c1 = outer(w2, w1, s, h)
    m1 = split(diag - 0.5 * c1)

    def both(x):
        return full(m1, full(m1, x).T)

    def both_rounded(x):
        x = x.astype(BF)
        x = (dot(m1[0], x) + dot(m1[1], x)).T.astype(BF)
        return dot(m1[0], x) + dot(m1[1], x)

    h2 = both(outer(hw2, hw, g1, h))
    h_ref[...] = h2
    s1 = both_rounded(c1)
    w2b = both_rounded(outer(w4, w3, w2, h))
    hh = h2.astype(BF)
    m2 = split(diag - 0.5 * outer(w2b, s1 - TAU * h2, s1, hh))

    p, i, r = panels(x_ref)
    hp = TAU * dot(h, p)
    hq = hp - (TAU * TAU) * dot(h, i)
    q = p.astype(F32) - TAU * i.astype(F32)
    t = q - TAU * r.astype(F32)
    psi1 = full(m1, q + hp)
    wpsi1 = full(m1, t + hq)
    psi2 = full(m2, wpsi1 + TAU * dot(hh, psi1.astype(BF))).astype(BF)
    group = psi_ref.shape[1]
    nh = x_ref.shape[1]
    for b in range(n // group):
        for h in range(nh):
            psi_ref[b * nh + h] = psi2[b * group : (b + 1) * group, h * BLK : (h + 1) * BLK]


def algebra(mine, theirs, x, volume, n_band):
    n = x.shape[2]
    count = n // n_band * x.shape[1]
    return call(
        functools.partial(algebra_kernel, volume),
        [jax.ShapeDtypeStruct((count, n_band, BLK), BF), jax.ShapeDtypeStruct((n, n), F32)],
        (mine, theirs, x),
        [pltpu.VMEM((NGRAM, n, n), F32), pltpu.VMEM((2 * mine.shape[0], BLK), F32)],
        48,
    )


def per_device(orbitals, potential):
    shape = orbitals.shape
    nb = shape[0]
    n_band = axes_size(BAND)
    cells = shape[1] * shape[2] * shape[3]
    bands = nb * n_band
    chunk = cells // n_band
    volume = 1.0 / (cells * lax.axis_size("dx") * lax.axis_size("dy"))

    send = images(orbitals, potential, n_band).transpose(1, 0, 2)
    got = swap(send, BAND).transpose(1, 0, 2)
    x = got.reshape(3, chunk // BLK, bands, BLK)

    count = bands // BLK * 2 * bands + len(pairs(bands // BLK)) * BLK
    halves = call(
        gram_kernel,
        [jax.ShapeDtypeStruct((count // 2, BLK), BF)] * 2,
        (x,),
        [pltpu.VMEM((count, BLK), BF)],
    )
    psi2, h2 = algebra(*reduced(*halves), x, volume, n_band)

    back = swap(psi2.transpose(1, 0, 2), BAND).transpose(1, 0, 2)
    mine = lax.dynamic_index_in_dim(h2.reshape(nb, n_band, bands), lax.axis_index(BAND), 1, False)
    columns = mine.reshape(nb, nb, n_band).transpose(2, 1, 0).reshape(bands, nb)
    return back.reshape(shape), columns


def solution(mesh):
    n_band, n_dx, n_dy = mesh.devices.shape
    near = min(2, n_band // 2)
    far = min(4, n_band // 2 // near)
    fine = Mesh(mesh.devices.reshape(-1, far, near, 2, n_dx, n_dy), BAND + ("dx", "dy"))
    in_specs = (P(BAND, "dx", "dy", None), P("dx", "dy", None))
    out_specs = (P(BAND, "dx", "dy", None), P(None, BAND))
    return jax.shard_map(
        per_device, mesh=fine, in_specs=in_specs, out_specs=out_specs, check_vma=False
    )
```

```python
import functools

import jax
import jax.numpy as jnp
import ml_dtypes
import numpy as np
from jax import lax
from jax.experimental import pallas as pl
from jax.experimental.pallas import tpu as pltpu
from jax.sharding import Mesh, PartitionSpec as P

COEFFS = (
    -5369.0 / 1800.0,
    12.0 / 7.0,
    -15.0 / 56.0,
    10.0 / 189.0,
    -1.0 / 112.0,
    2.0 / 1925.0,
    -1.0 / 16632.0,
)
TAU = 0.1
BF = jnp.bfloat16
F32 = jnp.float32
BAND = ("zhi", "yh", "yl", "core")
NEAR = ("dx", "dy", "yl")
BLK = 128
NGRAM = 5


def parts(matrix):
    high = matrix.astype(np.float32).astype(ml_dtypes.bfloat16)
    return high, (matrix - high.astype(np.float64)).astype(np.float32).astype(ml_dtypes.bfloat16)


def plane_matrix(out_rows, in_rows, wy):
    where = {row: k for k, row in enumerate(in_rows)}
    matrix = np.zeros((len(out_rows), len(in_rows)))
    for k, (side, x, y) in enumerate(out_rows):
        matrix[k, where[side, x, y]] += -1.5 * COEFFS[0]
        for offset in range(1, 7):
            for shift in (offset, -offset):
                matrix[k, where[side, x + shift, y]] += -0.5 * COEFFS[offset]
                at = (side * wy + y + shift) % (2 * wy)
                matrix[k, where[at // wy, x, at % wy]] += -0.5 * COEFFS[offset]
    return matrix


def line_matrix(length):
    matrix = np.zeros((length, length))
    at = np.arange(length)
    for offset in range(1, 7):
        for shift in (offset, -offset):
            matrix[at, (at + shift) % length] += -0.5 * COEFFS[offset]
    return matrix


def slab(side, first, last, wy):
    return [(side, x, y) for x in range(first, last) for y in range(wy)]


def hold_kernel(table_ref, held_ref):
    held_ref[...] = table_ref[...]


def edge_kernel(wide, p_ref, v_ref, other_ref, other_v_ref, last_ref, first_ref):
    nb, rows, _ = p_ref.shape
    narrow = last_ref.shape[1] - wide
    last_ref[:nb, :wide] = p_ref[:, rows - wide :]
    first_ref[:nb, :wide] = p_ref[:, :wide]
    last_ref[:nb, wide:] = other_ref[:, rows - narrow :]
    first_ref[:nb, wide:] = other_ref[:, :narrow]
    last_ref[nb, :wide] = v_ref[rows - wide :]
    first_ref[nb, :wide] = v_ref[:wide]
    last_ref[nb, wide:] = other_v_ref[rows - narrow :]
    first_ref[nb, wide:] = other_v_ref[:narrow]


def stencil_kernel(
    wide, p_ref, v_ref, other_ref, other_v_ref, lo_ref, hi_ref, table_ref, out_ref, field
):
    size = field.shape[0]
    nb, rows, _ = p_ref.shape
    narrow = lo_ref.shape[1] - wide
    middle = 2 * rows + 2 * narrow
    last = 2 * middle + rows
    end = last + rows
    corner = table_ref.shape[1] - BLK
    a1h, a1l = table_ref[:middle, :size], table_ref[middle : 2 * middle, :size]
    a2h, a2l = table_ref[2 * middle : last, :middle], table_ref[last:end, :middle]
    zh = table_ref[2 * middle : 2 * middle + BLK, corner:]
    zl = table_ref[2 * middle + BLK : 2 * middle + 2 * BLK, corner:]

    def along_z(x):
        halves = (x[:, :BLK], x[:, BLK:])
        return jnp.concatenate([dot(h, zh) + dot(h, zl) for h in halves], axis=1)

    def around(low, high, other):
        return jnp.concatenate([low[wide - narrow : wide], high[:narrow], other], axis=0).astype(F32)

    v = jnp.concatenate([v_ref[...], around(lo_ref[nb], hi_ref[nb], other_v_ref[...])], axis=0)
    v = jnp.concatenate([v, v], axis=1)
    chunks = out_ref.shape[1]
    parts_out = rows // chunks
    for b in range(0, nb, 2):
        at = 0
        for ref, first, size in (
            (p_ref, 0, rows), (lo_ref, 0, wide), (hi_ref, 0, wide),
            (other_ref, 0, rows), (lo_ref, wide, narrow), (hi_ref, wide, narrow),
        ):
            field[at : at + size, :BLK] = ref[b, first : first + size]
            field[at : at + size, BLK:] = ref[b + 1, first : first + size]
            at += size
        f = field[...]
        centre = jnp.concatenate(
            [
                f[:rows],
                f[rows + wide - narrow : rows + wide],
                f[rows + wide : rows + wide + narrow],
                f[rows + 2 * wide : 2 * rows + 2 * wide],
            ],
            axis=0,
        )
        image = dot(a1h, f) + dot(a1l, f) + along_z(centre)
        centre = centre.astype(F32)
        image = (image + v * centre).astype(BF)
        q = (centre - TAU * image.astype(F32)).astype(BF)
        own = q[:rows]
        second = dot(a2h, q) + dot(a2l, q) + along_z(own)
        second = (second + v[:rows] * own.astype(F32)).astype(BF)
        for k, x in enumerate((f[:rows], image[:rows], second)):
            for h in range(parts_out):
                for j in range(2):
                    block = x[h * chunks : (h + 1) * chunks, j * BLK : (j + 1) * BLK]
                    out_ref[(k * parts_out + h) * nb + b + j] = block


def call(kernel, outs, args, scratch=(), limit=32, cost=None):
    return pl.pallas_call(
        kernel,
        out_shape=tuple(outs),
        in_specs=[pl.BlockSpec(memory_space=pltpu.VMEM)] * len(args),
        out_specs=(pl.BlockSpec(memory_space=pltpu.VMEM),) * len(outs),
        scratch_shapes=list(scratch),
        cost_estimate=cost and pl.CostEstimate(flops=0, transcendentals=0, bytes_accessed=cost),
        compiler_params=pltpu.CompilerParams(vmem_limit_bytes=limit * 1024 * 1024),
    )(*args)


def images(orbitals, potential, chunks):
    nb, wx, wy, _ = orbitals.shape
    rows, wide, narrow = wx * wy, 12 * wy, 6 * wy
    p = orbitals.reshape(nb, rows, BLK)
    v = potential.reshape(rows, BLK)

    def shape(count, size):
        return jax.ShapeDtypeStruct((count, size, BLK), BF)

    whole = (
        slab(0, 0, wx, wy) + slab(0, -12, 0, wy) + slab(0, wx, wx + 12, wy)
        + slab(1, 0, wx, wy) + slab(1, -6, 0, wy) + slab(1, wx, wx + 6, wy)
    )
    middle = (
        slab(0, 0, wx, wy) + slab(0, -6, 0, wy) + slab(0, wx, wx + 6, wy) + slab(1, 0, wx, wy)
    )
    big = parts(plane_matrix(middle, whole, wy))
    small = parts(plane_matrix(slab(0, 0, wx, wy), middle, wy))
    line = parts(line_matrix(BLK))
    table = np.zeros((2 * len(middle) + 2 * max(rows, BLK), 5 * BLK), ml_dtypes.bfloat16)
    for k in range(2):
        table[k * len(middle) : (k + 1) * len(middle), : len(whole)] = big[k]
        at = 2 * len(middle) + k * rows
        table[at : at + rows, : len(middle)] = small[k]
        at = 2 * len(middle) + k * BLK
        table[at : at + BLK, -BLK:] = line[k]
    rounded = v.astype(BF)
    pair = [(0, 1), (1, 0)]
    other, other_v = lax.ppermute(p, "dy", pair), lax.ppermute(rounded, "dy", pair)
    (psi,) = call(hold_kernel, [shape(nb, rows)], (p,), cost=4 * p.size)
    (held,) = call(
        hold_kernel,
        [jax.ShapeDtypeStruct(table.shape, BF)],
        (jnp.asarray(table),),
        cost=4 * table.size,
    )
    last, first = call(
        functools.partial(edge_kernel, wide),
        [shape(nb + 1, wide + narrow)] * 2,
        (psi, rounded, other, other_v),
    )
    count = lax.axis_size("dx")
    up = [(k, (k + 1) % count) for k in range(count)]
    low = lax.ppermute(last, "dx", up)
    high = lax.ppermute(first, "dx", [(b, a) for a, b in up])
    return call(
        functools.partial(stencil_kernel, wide),
        [shape(3 * nb * rows // chunks, chunks)],
        (psi, v, other, other_v, low, high, held),
        [pltpu.VMEM((len(whole), 2 * BLK), BF)],
    )[0]


def swap(x, axes):
    return lax.all_to_all(x, axes, split_axis=0, concat_axis=0, tiled=True)


def spread(x, axes, size):
    return swap(jnp.broadcast_to(x[None], (size,) + x.shape), axes)


def pairs(nblk):
    return [(r, c) for r in range(nblk) for c in range(r, nblk)]


def tri(n):
    return lax.broadcasted_iota(jnp.int32, (n, n), 0), lax.broadcasted_iota(jnp.int32, (n, n), 1)


def panels(x_ref):
    return [
        jnp.concatenate([x_ref[k, h] for h in range(x_ref.shape[1])], axis=1) for k in range(3)
    ]


def core_halves(count):
    half = count // 2
    core = lax.axis_index("core")
    return [pl.ds(pl.multiple_of(c * half, BLK), half) for c in (core, 1 - core)]


def gram_kernel(x_ref, mine_ref, theirs_ref, rows_ref):
    p, i, r = panels(x_ref)
    n = p.shape[0]
    nblk = n // BLK
    qf = p.astype(F32) - TAU * i.astype(F32)
    q = qf.astype(BF)
    t = (qf - TAU * r.astype(F32)).astype(BF)

    def gram(a, b):
        return lax.dot_general(a, b, (((1,), (1,)), ((), ())), preferred_element_type=F32)

    s, g1, hw, hw2, w4 = gram(p, p), gram(i, p), gram(q, i), gram(r, q), gram(t, t)
    row, col = tri(n)
    at = 0
    for a, b in ((s, g1), (hw, hw2)):
        square = jnp.where(row > col, b, a).astype(BF)
        for c in range(nblk):
            rows_ref[at : at + n] = square[:, c * BLK : (c + 1) * BLK]
            at += n
    row, col = tri(BLK)

    def diagonal(g, k):
        block = g[k * BLK : (k + 1) * BLK, k * BLK : (k + 1) * BLK]
        return jnp.sum(jnp.where(row == col, block, 0.0), axis=0, keepdims=True)

    for k, c in pairs(nblk):
        block = w4[k * BLK : (k + 1) * BLK, c * BLK : (c + 1) * BLK]
        if k == c:
            first, second = diagonal(g1, k), diagonal(hw2, k)
            for at_row, line in (
                (BLK - 4, first), (BLK - 3, pltpu.roll(first, 64, 1)),
                (BLK - 2, second), (BLK - 1, pltpu.roll(second, 64, 1)),
            ):
                block = jnp.where((row == at_row) & (col < 64), line, block)
        rows_ref[at : at + BLK] = block.astype(BF)
        at += BLK
    mine, theirs = core_halves(rows_ref.shape[0])
    mine_ref[...] = rows_ref[mine]
    theirs_ref[...] = rows_ref[theirs]


def reduced(mine, theirs):
    n_near = axes_size(NEAR)
    pair = [(0, 1), (1, 0)]
    half = mine.astype(F32) + lax.ppermute(theirs, "core", pair).astype(F32)
    part = swap(half.astype(BF).reshape(n_near, -1, BLK), NEAR).astype(F32).sum(0)
    part = spread(part, "zhi", lax.axis_size("zhi")).sum(0)
    part = spread(part, "yh", lax.axis_size("yh")).sum(0)
    half = spread(part, NEAR, n_near).reshape(-1, BLK)
    return half, lax.ppermute(half, "core", pair)


def axes_size(axes):
    size = 1
    for axis in axes:
        size *= lax.axis_size(axis)
    return size


def dot(a, b):
    return jnp.dot(a, b, preferred_element_type=F32)


def split(x):
    high = x.astype(BF)
    return high, (x - high.astype(F32)).astype(BF)


def algebra_kernel(volume, mine_ref, theirs_ref, x_ref, psi_ref, h_ref, mats, rows_ref):
    n = x_ref.shape[2]
    nblk = n // BLK
    mine, theirs = core_halves(rows_ref.shape[0])
    rows_ref[mine] = mine_ref[...]
    rows_ref[theirs] = theirs_ref[...]
    row, col = tri(BLK)

    def put(g, r, c, tile):
        mats[g, r * BLK : (r + 1) * BLK, c * BLK : (c + 1) * BLK] = tile

    at = 2 * nblk * n
    lines = {}
    for r, c in pairs(nblk):
        tile = rows_ref[at : at + BLK] * volume
        at += BLK
        if r == c:
            for g, k in ((1, BLK - 4), (3, BLK - 2)):
                second = pltpu.roll(tile[k + 1 : k + 2], 64, 1)
                lines[g, r] = jnp.where(col[:1] < 64, tile[k : k + 1], second)
            put(4, r, r, jnp.where(row <= col, tile, tile.T))
        else:
            put(4, r, c, tile)
            put(4, c, r, tile.T)
    for g in (0, 2):
        for r in range(nblk):
            for c in range(nblk):
                at = (g // 2 * nblk + c) * n + r * BLK
                tile = rows_ref[at : at + BLK] * volume
                flip = tile.T
                if r == c:
                    put(g, r, r, jnp.where(row <= col, tile, flip))
                    other = jnp.where(row >= col, tile, flip)
                    put(g + 1, r, r, jnp.where(row == col, lines[g + 1, r], other))
                else:
                    to = g if r < c else g + 1
                    put(to, r, c, tile)
                    put(to, c, r, flip)
    s, g1, hw, hw2, w4 = (mats[g] for g in range(NGRAM))
    w1 = s - TAU * g1
    w2 = w1 - TAU * hw
    w3 = w2 - TAU * hw2
    row, col = tri(n)
    diag = jnp.where(row == col, 1.5, 0.0).astype(F32)

    def full(a, x):
        high, low = split(x)
        return dot(a[0], high) + dot(a[0], low) + dot(a[1], high)

    def outer(high, middle, low, h):
        b = middle + (0.5 * TAU) * dot(h, low.astype(BF))
        b = TAU * dot(b.astype(BF), h)
        return high + b + b.T

    h = g1.astype(BF)
    c1 = outer(w2, w1, s, h)
    m1 = split(diag - 0.5 * c1)

    def both(x):
        return full(m1, full(m1, x).T)

    def both_rounded(x):
        x = x.astype(BF)
        x = (dot(m1[0], x) + dot(m1[1], x)).T.astype(BF)
        return dot(m1[0], x) + dot(m1[1], x)

    h2 = both(outer(hw2, hw, g1, h))
    h_ref[...] = h2
    s1 = both_rounded(c1)
    w2b = both_rounded(outer(w4, w3, w2, h))
    hh = h2.astype(BF)
    m2 = split(diag - 0.5 * outer(w2b, s1 - TAU * h2, s1, hh))

    p, i, r = panels(x_ref)
    hp = TAU * dot(h, p)
    hq = hp - (TAU * TAU) * dot(h, i)
    q = p.astype(F32) - TAU * i.astype(F32)
    t = q - TAU * r.astype(F32)
    both_panels = full(m1, jnp.concatenate([q + hp, t + hq], axis=1))
    psi1, wpsi1 = both_panels[:, : q.shape[1]], both_panels[:, q.shape[1] :]
    psi2 = full(m2, wpsi1 + TAU * dot(hh, psi1.astype(BF))).astype(BF)
    group = psi_ref.shape[1]
    nh = x_ref.shape[1]
    for b in range(n // group):
        for h in range(nh):
            psi_ref[b * nh + h] = psi2[b * group : (b + 1) * group, h * BLK : (h + 1) * BLK]


def algebra(mine, theirs, x, volume, n_band):
    n = x.shape[2]
    count = n // n_band * x.shape[1]
    return call(
        functools.partial(algebra_kernel, volume),
        [jax.ShapeDtypeStruct((count, n_band, BLK), BF), jax.ShapeDtypeStruct((n, n), F32)],
        (mine, theirs, x),
        [pltpu.VMEM((NGRAM, n, n), F32), pltpu.VMEM((2 * mine.shape[0], BLK), F32)],
        48,
    )


def per_device(orbitals, potential):
    shape = orbitals.shape
    nb = shape[0]
    n_band = axes_size(BAND)
    cells = shape[1] * shape[2] * shape[3]
    bands = nb * n_band
    chunk = cells // n_band
    volume = 1.0 / (cells * lax.axis_size("dx") * lax.axis_size("dy"))

    send = images(orbitals, potential, n_band).transpose(1, 0, 2)
    got = swap(send, BAND).transpose(1, 0, 2)
    x = got.reshape(3, chunk // BLK, bands, BLK)

    count = bands // BLK * 2 * bands + len(pairs(bands // BLK)) * BLK
    halves = call(
        gram_kernel,
        [jax.ShapeDtypeStruct((count // 2, BLK), BF)] * 2,
        (x,),
        [pltpu.VMEM((count, BLK), BF)],
    )
    psi2, h2 = algebra(*reduced(*halves), x, volume, n_band)

    back = swap(psi2.transpose(1, 0, 2), BAND).transpose(1, 0, 2)
    mine = lax.dynamic_index_in_dim(h2.reshape(nb, n_band, bands), lax.axis_index(BAND), 1, False)
    columns = mine.reshape(nb, nb, n_band).transpose(2, 1, 0).reshape(bands, nb)
    return back.reshape(shape), columns


def solution(mesh):
    n_band, n_dx, n_dy = mesh.devices.shape
    near = min(2, n_band // 2)
    far = min(4, n_band // 2 // near)
    fine = Mesh(mesh.devices.reshape(-1, far, near, 2, n_dx, n_dy), BAND + ("dx", "dy"))
    in_specs = (P(BAND, "dx", "dy", None), P("dx", "dy", None))
    out_specs = (P(BAND, "dx", "dy", None), P(None, BAND))
    return jax.shard_map(
        per_device, mesh=fine, in_specs=in_specs, out_specs=out_specs, check_vma=False
    )
```
